128 devices in a mesh: seq: 32 (over x, z, core), head: 4 (over y).
Axes of the slice: x: 4, y: 4, z: 4, core: 2. Of those that a mesh axis runs over, the one named last changes fastest.
Arguments:
- values: bfloat16 [32768, 8192], P('seq', 'head'), may hold values from -6 to 6
- gate_rows: bfloat16 [32768, 8192], P('seq', 'head')
- input_map: bfloat16 [32768, 1024], P('seq', 'head'), may hold values from -1.5 to 1.5
- output_map: bfloat16 [32768, 1024], P('seq', 'head'), may hold values from -1.5 to 1.5
- decay_rate: bfloat16 [32768, 128], P('seq', 'head')
- step_size: bfloat16 [32768, 128], P('seq', 'head')
- skip_gain: float32 [128], P('head'), may hold values from 0.5 to 1.5
- norm_gain: float32 [8192], P('head'), may hold values from 0.5 to 1.5
- slot_map: int32 [4], replicated, may hold values from 0 to 127, as said below
- state_cache: bfloat16 [128, 128, 64, 256], P(('seq', 'head')), may hold values from -3 to 3
Outputs:
- mixed_rows: bfloat16 [32768, 8192], P('seq', 'head')
- new_cache: bfloat16 [128, 128, 64, 256], P(('seq', 'head'))
The draws below stay inside these ranges and needn't reach their ends.
Inputs may be any that keep to these rules, and one draw needn't show every extreme that they name: `slot_map`: the slot that receives a head group's final states; groups may share a slot.
All inputs are finite; a program needn't handle non-finite values.
Results may differ from the reference program's by a relative error of at most 0.0014.
The reference program's roundings to bfloat16 on the way count: a program that leaves them out, or rounds other values in their place, can miss the bound.
Values may be sent and summed in bfloat16 or wider, within the bound.
A program may use at most 256 MiB of HBM per device.

```python
import math
import jax
import jax.numpy as jnp
from jax import lax

HEADS = 128
HEAD_DIM = 64
STATE = 256
GROUPS = 4
SPAN = 256
TOK_DEV = 1024
PROMPT_TOKENS = 32768
SLOTS = 128


def head_memory(key, fast_tenths):
    head_kinds = jax.random.randint(jax.random.fold_in(key, 11), (HEADS,), 0, 10)
    quick_len = jax.random.uniform(jax.random.fold_in(key, 12), (HEADS,), minval=30.0, maxval=50.0)
    keep_share = jax.random.uniform(jax.random.fold_in(key, 13), (HEADS,), minval=0.15, maxval=0.6)
    return jnp.where(head_kinds < fast_tenths, quick_len, PROMPT_TOKENS / keep_share)


def draw_decay_rate(key, part):
    fast_tenths = 5
    retained_state = head_memory(key, fast_tenths)
    key = jax.random.fold_in(key, 3)
    jaggedness = jax.random.uniform(jax.random.fold_in(key, 1), (PROMPT_TOKENS, HEADS), minval=0.5, maxval=1.5)
    block_total = PROMPT_TOKENS // TOK_DEV
    block_multiplier = jnp.exp(jax.random.uniform(jax.random.fold_in(key, 5), (block_total, HEADS), minval=math.log(0.6), maxval=math.log(1.5)))
    block_multiplier = jnp.repeat(block_multiplier, TOK_DEV, axis=0)
    spike_position = jax.random.randint(jax.random.fold_in(key, 2), (3,), 0, PROMPT_TOKENS)
    intensity = jax.random.uniform(jax.random.fold_in(key, 4), (3,), minval=0.22, maxval=0.45)
    spike_count = (jnp.arange(PROMPT_TOKENS)[:, None] == spike_position[None, :]).astype(jnp.float32)
    spike_total = jnp.sum(spike_count * intensity[None, :], axis=1)
    return (jaggedness * block_multiplier / retained_state[None, :] + spike_total[:, None]).astype(jnp.bfloat16)


def draw_step_size(key, part):
    fast_tenths = 5
    retained_state = head_memory(key, fast_tenths)
    key = jax.random.fold_in(key, 5)
    jaggedness = jax.random.uniform(key, (PROMPT_TOKENS, HEADS), minval=0.5, maxval=1.5)
    return (jaggedness * jax.lax.rsqrt(retained_state)[None, :]).astype(jnp.bfloat16)


def draw_gate_rows(key, part):
    key = jax.random.fold_in(key, 7)
    gaussian = jax.random.normal(jax.random.fold_in(key, 1), (PROMPT_TOKENS, HEADS * HEAD_DIM))
    scale_low = 0.4
    scale_high = 4.0
    row_scale = jnp.exp(jax.random.uniform(jax.random.fold_in(key, 3), (PROMPT_TOKENS, 1), minval=math.log(scale_low), maxval=math.log(scale_high)))
    column_scale = jnp.exp(jax.random.uniform(jax.random.fold_in(key, 4), (1, HEADS * HEAD_DIM), minval=math.log(scale_low), maxval=math.log(scale_high)))
    return (gaussian * row_scale * column_scale).astype(jnp.bfloat16)


def draw_slot_map(key, part):
    key = jax.random.fold_in(key, 9)
    chosen = jax.random.randint(jax.random.fold_in(key, 1), (GROUPS,), 0, SLOTS)
    top_pos = jax.random.randint(jax.random.fold_in(key, 2), (), 0, GROUPS)
    bottom_pos = (top_pos + 1 + jax.random.randint(jax.random.fold_in(key, 3), (), 0, GROUPS - 1)) % GROUPS
    position = jnp.arange(GROUPS)
    chosen = jnp.where(position == top_pos, SLOTS - 1, jnp.where(position == bottom_pos, 0, chosen))
    return chosen.astype(jnp.int32)


def levels(own_key, shape, shards, least, largest):
    loudness = 1.0
    for dim, parts in shards:
        heights = jax.random.uniform(jax.random.fold_in(jax.random.fold_in(own_key, 6), dim), (parts,), jnp.float32, least / len(shards), largest / len(shards))
        loudness = loudness * jnp.repeat(jnp.exp(heights), shape[dim] // parts).reshape((-1,) + (1,) * (len(shape) - 1 - dim))
    return loudness


def noise(key, extent, scale, most, split=(), held_as=jnp.bfloat16):
    factor_of = levels(key, extent, split, -0.22, 0.18) if split else 1.0
    values = jax.random.normal(key, extent, jnp.float32) * scale * factor_of
    return jnp.minimum(jnp.maximum(values, -most), most).astype(held_as)


def setup_inputs(seed: int = 0) -> dict:
    keys = jax.random.split(jax.random.key(seed), 11)
    return {
        "values": noise(keys[0], (PROMPT_TOKENS, HEADS * HEAD_DIM), 1.0, 6.0, ((0, 32), (1, 4))),
        "gate_rows": draw_gate_rows(jax.random.fold_in(keys[10], 71), 0),
        "input_map": noise(keys[2], (PROMPT_TOKENS, GROUPS * STATE), 0.25, 1.5, ((0, 32), (1, 4))),
        "output_map": noise(keys[3], (PROMPT_TOKENS, GROUPS * STATE), 0.25, 1.5, ((0, 32), (1, 4))),
        "decay_rate": draw_decay_rate(jax.random.fold_in(keys[10], 71), 0),
        "step_size": draw_step_size(jax.random.fold_in(keys[10], 71), 0),
        "skip_gain": jnp.clip(0.5 + 1.0 * jax.random.uniform(keys[6], (HEADS,), jnp.float32) ** levels(keys[6], (HEADS,), ((0, 4),), -0.2, 0.2), 0.5, 1.5),
        "norm_gain": jnp.clip(1.0 + 0.1 * jax.random.normal(keys[7], (HEADS * HEAD_DIM,), jnp.float32), 0.5, 1.5),
        "slot_map": draw_slot_map(jax.random.fold_in(keys[10], 71), 0),
        "state_cache": noise(keys[9], (SLOTS, HEADS, HEAD_DIM, STATE), 0.5, 3.0, ((0, 128),)),
    }


HIGHEST = lax.Precision.HIGHEST

def to_half_wide(array):
    half = lax.optimization_barrier(array.astype(jnp.bfloat16))
    return half.astype(jnp.float32)

def block_scan(block_values, block_rates, block_steps, block_in, block_out):
    length, heads_here, head_width = block_values.shape
    group_count = block_in.shape[1]
    state_width = block_in.shape[2]
    per_group = heads_here // group_count
    block_rows = SPAN
    block_count = length // block_rows
    causal = jnp.arange(block_rows)[:, None] >= jnp.arange(block_rows)[None, :]

    def advance(carry_state, block_items):
        vals, rates, steps, maps_in, maps_out = block_items
        widened = vals.astype(jnp.float32)
        wide_in = maps_in.astype(jnp.float32)
        wide_out = maps_out.astype(jnp.float32)
        running = jnp.cumsum(rates, axis=0)
        running_t = running.T
        spread = running_t[:, :, None] - running_t[:, None, :]
        pair_decay = jnp.where(causal, jnp.exp(-jnp.where(causal, spread, 0.0)), 0.0)
        inner_prod = jnp.einsum('ign,jgn->gij', wide_out, wide_in, precision=HIGHEST)
        weight = inner_prod[:, None] * pair_decay.reshape(group_count, per_group, block_rows, block_rows)
        weight = weight * steps.T.reshape(group_count, per_group, 1, block_rows)
        weight = to_half_wide(weight.reshape(heads_here, block_rows, block_rows))
        inside = jnp.einsum('kij,jkp->ikp', weight, widened, precision=HIGHEST)
        entry_half = to_half_wide(carry_state).reshape(group_count, per_group * head_width, state_width)
        carried = jnp.einsum('ign,gqn->igq', wide_out, entry_half, precision=HIGHEST)
        carried = carried.reshape(block_rows, heads_here, head_width) * jnp.exp(-running)[:, :, None]
        trailing = jnp.exp(-(running[-1:] - running)) * steps
        scaled_in = trailing.reshape(block_rows, group_count, per_group)[:, :, :, None] * wide_in[:, :, None, :]
        scaled_in = to_half_wide(scaled_in)
        state_add = jnp.einsum('jgqp,jgqn->gqpn', widened.reshape(block_rows, group_count, per_group, head_width), scaled_in, precision=HIGHEST)
        state_add = state_add.reshape(heads_here, head_width, state_width)
        carry_state = jnp.exp(-running[-1])[:, None, None] * carry_state + state_add
        return (carry_state, inside + carried)
    block_items = (block_values.reshape(block_count, block_rows, heads_here, head_width), block_rates.reshape(block_count, block_rows, heads_here), block_steps.reshape(block_count, block_rows, heads_here), block_in.reshape(block_count, block_rows, group_count, state_width), block_out.reshape(block_count, block_rows, group_count, state_width))
    zero_state = jnp.zeros((heads_here, head_width, state_width), jnp.float32)
    last_state, outputs = lax.scan(advance, zero_state, block_items)
    return (outputs.reshape(length, heads_here, head_width), last_state)

def reference(values, gate_rows, input_map, output_map, decay_rate, step_size, skip_gain, norm_gain, slot_map, state_cache):
    per_group = HEADS // GROUPS
    seq_rows, last_state = block_scan(values.reshape(PROMPT_TOKENS, HEADS, HEAD_DIM), decay_rate.astype(jnp.float32), step_size.astype(jnp.float32), input_map.reshape(PROMPT_TOKENS, GROUPS, STATE), output_map.reshape(PROMPT_TOKENS, GROUPS, STATE))
    ssd_rows = seq_rows.astype(jnp.bfloat16).reshape(PROMPT_TOKENS, HEADS * HEAD_DIM)
    summed = ssd_rows.astype(jnp.float32) + values.astype(jnp.float32) * jnp.repeat(skip_gain, HEAD_DIM)[None, :]
    gated = summed * jax.nn.silu(gate_rows.astype(jnp.float32))
    grouped = gated.reshape(PROMPT_TOKENS, GROUPS, per_group * HEAD_DIM)
    inverse_rms = lax.rsqrt(lax.optimization_barrier(jnp.mean(grouped * grouped, axis=2, keepdims=True)) + 1e-05)
    mixed_rows = ((grouped * inverse_rms).reshape(PROMPT_TOKENS, HEADS * HEAD_DIM) * norm_gain[None, :]).astype(jnp.bfloat16)
    head_group = jnp.arange(HEADS, dtype=jnp.int32) // per_group
    wanted = slot_map[head_group]
    matched = jnp.arange(SLOTS, dtype=jnp.int32)[:, None] == wanted[None, :]
    new_cache = jnp.where(matched[:, :, None, None], last_state.astype(jnp.bfloat16)[None], state_cache)
    return (mixed_rows, new_cache)
```

```python
import functools

import jax
import jax.numpy as jnp
from jax import lax
from jax.experimental import pallas as pl
from jax.experimental.pallas import tpu as pltpu
from jax.sharding import PartitionSpec as P

MESH = pl.DeviceIdType.MESH
F32 = jnp.float32
BF16 = jnp.bfloat16

HEADS = 128
HEAD_DIM = 64
STATE = 256
GROUPS = 4
SPAN = 256
BLOCKS = 4
TOKENS = SPAN * BLOCKS
LOCAL_HEADS = 32
PAIRS = 16
CHIPS = 16
HALF = 128
ROWS = HALF + 8
WIDE = PAIRS * 128
LOG2E = 1.4426950408889634
LAG = 2
EARLY = 9


def dot(a, b):
    return jnp.dot(a, b, preferred_element_type=F32)


def lanes_of(p):
    return pl.ds(pl.multiple_of(p * 128, 128), 128)


def mixer_kernel(
    values, gate, b_ref, c_ref, rates, steps, skip, gain,
    mixed, gath,
    xv, zv, adds, ins, fac, sbuf, prt, cbuf, own_in, ebuf, ent_in, mbuf, pin, entry,
    bt, ip, rcol, run_t, step_t, trail_t, dwide, dec, ddec, sq, ob, fin,
    xsem, zsem, ps_s, ps_r, os_s, os_r, en_s, en_r, ms_s, ms_r,
    gl_s, gz_s, gz_r, gx_s, gx_r, gy_s, gy_r, gp_s, gp_r, out_sem,
):
    seq = lax.axis_index("seq")
    y = lax.axis_index("head")
    c = seq // 2
    k = lax.rem(seq, 2)
    zc = lax.rem(c, 4)
    xc = c // 4
    partner = 2 * c + 1 - k
    first = k == 0

    barrier = pltpu.get_barrier_semaphore()
    pl.semaphore_signal(barrier, inc=1, device_id={"seq": partner}, device_id_type=MESH)

    def greet(i, _):
        peer = lax.rem(c + 1 + i, CHIPS)
        pl.semaphore_signal(barrier, inc=1, device_id={"seq": 2 * peer + k}, device_id_type=MESH)
        return 0

    lax.fori_loop(0, CHIPS - 1, greet, 0)
    for j in range(1, GROUPS):
        pl.semaphore_signal(
            barrier, inc=1, device_id={"head": lax.rem(y + j, GROUPS)}, device_id_type=MESH
        )

    def x_copy(p):
        return pltpu.make_async_copy(values.at[:, lanes_of(p)], xv.at[:, lanes_of(p)], xsem.at[p])

    def start_x(i, _):
        x_copy(lax.rem(c + 1 + i, CHIPS)).start()
        return 0

    lax.fori_loop(0, PAIRS, start_x, 0)
    z_copy = pltpu.make_async_copy(gate, zv, zsem)
    z_copy.start()

    lane = lax.broadcasted_iota(jnp.int32, (SPAN, 128), 1)
    low = lane < 64
    upper = (
        lax.broadcasted_iota(jnp.int32, (SPAN, SPAN), 0)
        <= lax.broadcasted_iota(jnp.int32, (SPAN, SPAN), 1)
    ).astype(BF16)
    low16 = lax.broadcasted_iota(jnp.int32, (PAIRS, 128), 1) < 64
    for b in range(BLOCKS):
        rows = slice(b * SPAN, (b + 1) * SPAN)
        run_b = dot(rates[:, rows], upper) * LOG2E
        step_b = steps[:, rows].astype(F32)
        fill = jnp.zeros((128 - LOCAL_HEADS, SPAN), F32)
        rcol[rows, :] = jnp.concatenate([run_b, fill], axis=0).T
        total = run_b[:, SPAN - 1 : SPAN]
        run_t[:, rows] = run_b
        step_t[:, rows] = step_b
        trail_t[:, rows] = jnp.exp2(run_b - total) * step_b
        dwide[...] = jnp.broadcast_to(jnp.exp2(-total), (LOCAL_HEADS, 128))
        part = jnp.where(low16, dwide[pl.ds(0, PAIRS, 2), :], dwide[pl.ds(1, PAIRS, 2), :])
        dec[b] = part
        ddec[...] = part if b == 0 else ddec[...] * part
        bt[b] = b_ref[rows, :].astype(F32).T
        ip[b] = lax.dot_general(
            c_ref[rows, :], b_ref[rows, :], (((1,), (1,)), ((), ())), preferred_element_type=F32
        )

    pl.semaphore_wait(barrier, 1 + (CHIPS - 1) + (GROUPS - 1))

    def partner_copy(p):
        return pltpu.make_async_remote_copy(
            src_ref=sbuf.at[p, 1 - k], dst_ref=prt.at[p], send_sem=ps_s.at[p], recv_sem=ps_r.at[p],
            device_id={"seq": partner}, device_id_type=MESH,
        )

    def owner_copy(p):
        return pltpu.make_async_remote_copy(
            src_ref=cbuf.at[p], dst_ref=own_in.at[c], send_sem=os_s.at[p], recv_sem=os_r.at[c],
            device_id={"seq": 2 * p + k}, device_id_type=MESH,
        )

    def owner_arrival(j):
        return pltpu.make_async_remote_copy(
            src_ref=cbuf.at[j], dst_ref=own_in.at[j], send_sem=os_s.at[j], recv_sem=os_r.at[j],
            device_id={"seq": 2 * j + k}, device_id_type=MESH,
        )

    def states(p):
        x_copy(p).wait()
        ln = lanes_of(p)
        state = None
        for b in range(BLOCKS):
            rows = slice(b * SPAN, (b + 1) * SPAN)
            x = xv[rows, ln]
            x0 = jnp.where(low, x, jnp.zeros_like(x))
            x1 = jnp.where(low, jnp.zeros_like(x), x)
            wide = bt[b]
            s0 = (wide * trail_t[pl.ds(2 * p, 1), rows]).astype(BF16)
            s1 = (wide * trail_t[pl.ds(2 * p + 1, 1), rows]).astype(BF16)
            add = dot(s0, x0) + dot(s1, x1)
            if b < BLOCKS - 1:
                adds[b, :, ln] = add
            state = add if b == 0 else state * dec[b, pl.ds(p, 1), :] + add
        decay = jnp.broadcast_to(ddec[pl.ds(p, 1), :], (8, 128))
        for h in range(2):
            sbuf[p, h, 0:HALF, :] = state[h * HALF : (h + 1) * HALF]
            sbuf[p, h, HALF:ROWS, :] = decay
        partner_copy(p).start()

    def combine(p):
        partner_copy(p).wait_recv()
        here = sbuf[p, k]
        there = prt[p]
        early = jnp.where(first, here, there)
        late = jnp.where(first, there, here)
        decay = late[HALF : HALF + 1, :]
        return early[0:HALF] * decay + late[0:HALF], early[HALF:ROWS] * late[HALF:ROWS]

    def send_owner(p):
        both, decay = combine(p)
        cbuf[p, 0:HALF, :] = both
        cbuf[p, HALF:ROWS, :] = decay
        owner_copy(p).start()

    def states_step(i, _):
        states(lax.rem(c + 1 + i, CHIPS))

        @pl.when(i >= LAG)
        def _():
            send_owner(lax.rem(c + 1 + i - LAG, CHIPS))

        return 0

    lax.fori_loop(0, PAIRS, states_step, 0)

    def tail_step(i, _):
        send_owner(lax.rem(c + 1 + i, CHIPS))
        return 0

    lax.fori_loop(PAIRS - LAG, PAIRS - 1, tail_step, 0)
    both, decay = combine(c)
    own_in[c, 0:HALF, :] = both
    own_in[c, HALF:ROWS, :] = decay

    tri = (
        lax.broadcasted_iota(jnp.int32, (128, 128), 0)
        >= lax.broadcasted_iota(jnp.int32, (128, 128), 1)
    )

    def inner(p, _):
        ln = lanes_of(p)
        shift = lax.rem(128 - 2 * p, 128)
        for b in range(BLOCKS):
            r0 = b * SPAN
            rows = slice(r0, r0 + SPAN)
            turned = pltpu.roll(rcol[rows, :], shift, 1)
            cols = [jnp.broadcast_to(turned[:, h : h + 1], (SPAN, 128)) for h in range(2)]
            fac[rows, ln] = jnp.exp2(-jnp.where(low, cols[0], cols[1]))
            x = xv[rows, ln]
            top = bottom = None
            for h in range(2):
                xh = jnp.where(low, x, jnp.zeros_like(x)) if h == 0 else jnp.where(low, jnp.zeros_like(x), x)
                ru = run_t[pl.ds(2 * p + h, 1), rows]
                st = step_t[pl.ds(2 * p + h, 1), rows]
                rt = cols[h]
                w00 = jnp.where(tri, jnp.exp2(ru[:, :128] - rt[:128]), 0.0) * ip[b, :128, :128] * st[:, :128]
                w10 = jnp.exp2(ru[:, :128] - rt[128:]) * ip[b, 128:, :128] * st[:, :128]
                w11 = jnp.where(tri, jnp.exp2(ru[:, 128:] - rt[128:]), 0.0) * ip[b, 128:, 128:] * st[:, 128:]
                t = dot(w00.astype(BF16), xh[:128])
                u = dot(jnp.concatenate([w10.astype(BF16), w11.astype(BF16)], axis=1), xh)
                top = t if top is None else top + t
                bottom = u if bottom is None else bottom + u
            ins[r0 : r0 + 128, ln] = top
            ins[r0 + 128 : r0 + 256, ln] = bottom
        return 0

    lax.fori_loop(0, EARLY, inner, 0)

    def scan_step(j, state):
        @pl.when(j != c)
        def _():
            owner_arrival(j).wait_recv()

        ebuf[j] = state
        return state * own_in[j, HALF : HALF + 1, :] + own_in[j, 0:HALF, :]

    last = lax.fori_loop(0, CHIPS, scan_step, jnp.zeros((HALF, 128), F32))
    fin[...] = last.T.astype(BF16)

    def z_send(j):
        to = xc * 4 + lax.rem(zc + j, 4)
        return pltpu.make_async_remote_copy(
            src_ref=fin, dst_ref=gath.at[k, y, c], send_sem=gz_s.at[j - 1], recv_sem=gz_r.at[j - 1],
            device_id={"seq": 2 * to + k}, device_id_type=MESH,
        )

    def z_arrival(j):
        src = xc * 4 + lax.rem(zc + 4 - j, 4)
        return pltpu.make_async_remote_copy(
            src_ref=fin, dst_ref=gath.at[k, y, src], send_sem=gz_s.at[j - 1], recv_sem=gz_r.at[j - 1],
            device_id={"seq": 2 * src + k}, device_id_type=MESH,
        )

    keep = pltpu.make_async_copy(fin, gath.at[k, y, c], gl_s)
    keep.start()
    for j in range(1, 4):
        z_send(j).start()

    def entry_copy(j):
        return pltpu.make_async_remote_copy(
            src_ref=ebuf.at[j], dst_ref=ent_in.at[c], send_sem=en_s.at[j], recv_sem=en_r.at[c],
            device_id={"seq": 2 * j + k}, device_id_type=MESH,
        )

    def entry_arrival(p):
        return pltpu.make_async_remote_copy(
            src_ref=ebuf.at[p], dst_ref=ent_in.at[p], send_sem=en_s.at[p], recv_sem=en_r.at[p],
            device_id={"seq": 2 * p + k}, device_id_type=MESH,
        )

    def send_entry(i, _):
        entry_copy(lax.rem(c + 1 + i, CHIPS)).start()
        return 0

    lax.fori_loop(0, CHIPS - 1, send_entry, 0)
    ent_in[c] = ebuf[c]

    lax.fori_loop(EARLY, PAIRS, inner, 0)

    def x_send(j):
        to = lax.rem(xc + j, 4) * 4 + zc
        return pltpu.make_async_remote_copy(
            src_ref=gath.at[k, y, pl.ds(xc * 4, 4)], dst_ref=gath.at[k, y, pl.ds(xc * 4, 4)],
            send_sem=gx_s.at[j - 1], recv_sem=gx_r.at[j - 1],
            device_id={"seq": 2 * to + k}, device_id_type=MESH,
        )

    def x_arrival(j):
        src = lax.rem(xc + 4 - j, 4)
        return pltpu.make_async_remote_copy(
            src_ref=gath.at[k, y, pl.ds(src * 4, 4)], dst_ref=gath.at[k, y, pl.ds(src * 4, 4)],
            send_sem=gx_s.at[j - 1], recv_sem=gx_r.at[j - 1],
            device_id={"seq": 2 * (src * 4 + zc) + k}, device_id_type=MESH,
        )

    keep.wait()
    for j in range(1, 4):
        z_arrival(j).wait_recv()
    for j in range(1, 4):
        x_send(j).start()

    def entry_to_partner(p):
        return pltpu.make_async_remote_copy(
            src_ref=mbuf.at[p], dst_ref=pin.at[p], send_sem=ms_s.at[p], recv_sem=ms_r.at[p],
            device_id={"seq": partner}, device_id_type=MESH,
        )

    z_copy.wait()
    sq[...] = jnp.zeros_like(sq)

    def receive(p):
        @pl.when(p != c)
        def _():
            entry_arrival(p).wait_recv()

        state = ent_in[p]
        early = jnp.where(first, sbuf[p, 0], prt[p])
        moved = state * early[HALF : HALF + 1, :] + early[0:HALF]
        entry[pl.ds(pl.multiple_of(k * HALF, HALF), HALF), lanes_of(p)] = jnp.where(first, state, moved)
        mbuf[p] = jnp.where(first, moved, state)
        entry_to_partner(p).start()

    def finish(p):
        ln = lanes_of(p)
        entry_to_partner(p).wait_recv()
        entry[pl.ds(pl.multiple_of((1 - k) * HALF, HALF), HALF), ln] = pin[p]
        state = entry[:, ln]
        skip_row = jnp.where(low[0:1], skip[2 * p], skip[2 * p + 1])
        for b in range(BLOCKS):
            rows = slice(b * SPAN, (b + 1) * SPAN)
            carried = dot(c_ref[rows, :], state.astype(BF16))
            ssd = (ins[rows, ln] + carried * fac[rows, ln]).astype(BF16).astype(F32)
            z = zv[rows, ln].astype(F32)
            gated = (ssd + xv[rows, ln].astype(F32) * skip_row) * (z / (1.0 + jnp.exp(-z)))
            ins[rows, ln] = gated
            sq[rows, :] = sq[rows, :] + gated * gated
            if b < BLOCKS - 1:
                state = state * dec[b, pl.ds(p, 1), :] + adds[b, :, ln]

    def finish_step(i, _):
        @pl.when(i < PAIRS)
        def _():
            receive(lax.rem(c + CHIPS - i, CHIPS))

        @pl.when(i >= LAG)
        def _():
            finish(lax.rem(c + CHIPS + LAG - i, CHIPS))

        return 0

    def y_send(j):
        return pltpu.make_async_remote_copy(
            src_ref=gath.at[k, y], dst_ref=gath.at[k, y], send_sem=gy_s.at[j - 1], recv_sem=gy_r.at[j - 1],
            device_id={"head": lax.rem(y + j, 4)}, device_id_type=MESH,
        )

    def y_arrival(j):
        src = lax.rem(y + 4 - j, 4)
        return pltpu.make_async_remote_copy(
            src_ref=gath.at[k, src], dst_ref=gath.at[k, src], send_sem=gy_s.at[j - 1], recv_sem=gy_r.at[j - 1],
            device_id={"head": src}, device_id_type=MESH,
        )

    def p_send(j):
        at = lax.rem(y + 4 - j, 4)
        return pltpu.make_async_remote_copy(
            src_ref=gath.at[k, at], dst_ref=gath.at[k, at], send_sem=gp_s.at[j], recv_sem=gp_r.at[j],
            device_id={"seq": partner}, device_id_type=MESH,
        )

    def p_arrival(j):
        at = lax.rem(y + 4 - j, 4)
        return pltpu.make_async_remote_copy(
            src_ref=gath.at[1 - k, at], dst_ref=gath.at[1 - k, at], send_sem=gp_s.at[j], recv_sem=gp_r.at[j],
            device_id={"seq": partner}, device_id_type=MESH,
        )

    lax.fori_loop(0, 7, finish_step, 0)
    for j in range(1, 4):
        x_arrival(j).wait_recv()
    for j in range(1, 4):
        y_send(j).start()
    p_send(0).start()
    lax.fori_loop(7, PAIRS + LAG, finish_step, 0)

    def out_copy(b):
        rows = pl.ds(b * SPAN, SPAN)
        return pltpu.make_async_copy(ob.at[rows, :], mixed.at[rows, :], out_sem.at[b])

    for b in range(BLOCKS):
        rows = slice(b * SPAN, (b + 1) * SPAN)
        mean = jnp.sum(sq[rows, :], axis=1, keepdims=True) * (1.0 / WIDE)
        inverse = jnp.broadcast_to(lax.rsqrt(mean + 1e-05), (SPAN, 128))

        def norm_step(p, _, rows=rows, inverse=inverse):
            ln = lanes_of(p)
            ob[rows, ln] = (ins[rows, ln] * inverse * gain[pl.ds(p, 1), :]).astype(BF16)
            return 0

        lax.fori_loop(0, PAIRS, norm_step, 0)
        out_copy(b).start()

    for j in (1, 3, 2):
        y_arrival(j).wait_recv()
        p_send(j).start()
    for b in range(BLOCKS):
        out_copy(b).wait()
    for j in range(1, 4):
        z_send(j).wait_send()
        x_send(j).wait_send()
        y_send(j).wait_send()
    for j in range(4):
        p_send(j).wait_send()
        p_arrival(j).wait_recv()

    def drain(p, _):
        partner_copy(p).wait_send()
        entry_to_partner(p).wait_send()

        @pl.when(p != c)
        def _():
            owner_copy(p).wait_send()
            entry_copy(p).wait_send()

        return 0

    lax.fori_loop(0, PAIRS, drain, 0)


def run_mixer(values, gate, input_map, output_map, rates, steps, skip, gain):
    vm = lambda *shape: pltpu.VMEM(shape, F32)
    dma = lambda *shape: pltpu.SemaphoreType.DMA(shape)
    any_spec = pl.BlockSpec(memory_space=pl.ANY)
    vmem_spec = pl.BlockSpec(memory_space=pltpu.VMEM)
    return pl.pallas_call(
        mixer_kernel,
        out_shape=(
            jax.ShapeDtypeStruct((TOKENS, WIDE), BF16),
            jax.ShapeDtypeStruct((2, GROUPS, CHIPS, 128, 128), BF16),
        ),
        in_specs=[any_spec, any_spec] + [vmem_spec] * 4 + [pl.BlockSpec(memory_space=pltpu.SMEM), vmem_spec],
        out_specs=(any_spec, any_spec),
        scratch_shapes=[
            pltpu.VMEM((TOKENS, WIDE), BF16),
            pltpu.VMEM((TOKENS, WIDE), BF16),
            vm(BLOCKS - 1, STATE, WIDE),
            vm(TOKENS, WIDE),
            vm(TOKENS, WIDE),
            vm(PAIRS, 2, ROWS, 128),
            vm(PAIRS, ROWS, 128),
            vm(PAIRS, ROWS, 128),
            vm(CHIPS, ROWS, 128),
            vm(CHIPS, HALF, 128),
            vm(PAIRS, HALF, 128),
            vm(PAIRS, HALF, 128),
            vm(PAIRS, HALF, 128),
            vm(STATE, WIDE),
            vm(BLOCKS, STATE, SPAN),
            vm(BLOCKS, SPAN, SPAN),
            vm(TOKENS, 128),
            vm(LOCAL_HEADS, TOKENS),
            vm(LOCAL_HEADS, TOKENS),
            vm(LOCAL_HEADS, TOKENS),
            vm(LOCAL_HEADS, 128),
            vm(BLOCKS, PAIRS, 128),
            vm(PAIRS, 128),
            vm(TOKENS, 128),
            pltpu.VMEM((TOKENS, WIDE), BF16),
            pltpu.VMEM((128, HALF), BF16),
            dma(PAIRS), pltpu.SemaphoreType.DMA,
            dma(PAIRS), dma(PAIRS),
            dma(PAIRS), dma(PAIRS),
            dma(PAIRS), dma(PAIRS),
            dma(PAIRS), dma(PAIRS),
            pltpu.SemaphoreType.DMA,
            dma(3), dma(3), dma(3), dma(3), dma(3), dma(3), dma(4), dma(4),
            dma(BLOCKS),
        ],
        compiler_params=pltpu.CompilerParams(
            collective_id=0, has_side_effects=True, vmem_limit_bytes=60 * 1024 * 1024
        ),
        cost_estimate=pl.CostEstimate(flops=6_000_000_000, bytes_accessed=24_000_000, transcendentals=12_000_000),
        name="mixer",
    )(values, gate, input_map, output_map, rates, steps, skip, gain)


def place_kernel(slot_map, cache, gath, rows_in, out, rows_out, cbuf, rbuf, cin, cout, rin, rout):
    rank = lax.axis_index("seq") * GROUPS + lax.axis_index("head")

    def rows_step(b, start):
        rows = pl.ds(b * SPAN, SPAN)
        if start:
            return pltpu.make_async_copy(rows_in.at[rows], rbuf.at[rows], rin.at[b])
        return pltpu.make_async_copy(rbuf.at[rows], rows_out.at[rows], rout.at[b])

    def cache_in(g, h):
        part = pl.ds(h * 8, 8)
        return pltpu.make_async_copy(cache.at[g, part], cbuf.at[g, part], cin.at[2 * g + h])

    def cache_out(g, h):
        part = pl.ds(h * 8, 8)
        return pltpu.make_async_copy(cbuf.at[g, part], out.at[g, part], cout.at[2 * g + h])

    for g in range(GROUPS):
        hit = slot_map[g] == rank

        @pl.when(hit)
        def _(g=g):
            for h in range(2):
                pltpu.make_async_copy(
                    gath.at[h, g], cbuf.at[g, :, :, pl.ds(h * HALF, HALF)], cin.at[2 * g + h]
                ).start()

        @pl.when(jnp.logical_not(hit))
        def _(g=g):
            for h in range(2):
                cache_in(g, h).start()

        rows_step(g, True).start()

    for g in range(GROUPS):
        for h in range(2):
            cache_in(g, h).wait()
        for h in range(2):
            cache_out(g, h).start()
        rows_step(g, True).wait()
        rows_step(g, False).start()
    for g in range(GROUPS):
        for h in range(2):
            cache_out(g, h).wait()
        rows_step(g, False).wait()


def run_place(slot_map, cache, gath, rows):
    any_spec = pl.BlockSpec(memory_space=pl.ANY)
    return pl.pallas_call(
        place_kernel,
        out_shape=(
            jax.ShapeDtypeStruct((GROUPS, PAIRS, 128, STATE), BF16),
            jax.ShapeDtypeStruct((TOKENS, WIDE), BF16),
        ),
        in_specs=[pl.BlockSpec(memory_space=pltpu.SMEM), any_spec, any_spec, any_spec],
        out_specs=(any_spec, any_spec),
        scratch_shapes=[
            pltpu.VMEM((GROUPS, PAIRS, 128, STATE), BF16),
            pltpu.VMEM((TOKENS, WIDE), BF16),
            pltpu.SemaphoreType.DMA((2 * GROUPS,)),
            pltpu.SemaphoreType.DMA((2 * GROUPS,)),
            pltpu.SemaphoreType.DMA((BLOCKS,)),
            pltpu.SemaphoreType.DMA((BLOCKS,)),
        ],
        compiler_params=pltpu.CompilerParams(vmem_limit_bytes=60 * 1024 * 1024),
        name="place",
    )(slot_map, cache, gath, rows)


def shards(
    values, gate_rows, input_map, output_map, decay_rate, step_size, skip_gain, norm_gain, slot_map, state_cache
):
    gain = norm_gain.reshape(PAIRS, 128)
    rows, gath = run_mixer(
        values, gate_rows, input_map, output_map, decay_rate.T, step_size.T, skip_gain, gain
    )
    cache = state_cache.reshape(GROUPS, PAIRS, 128, STATE)
    new_cache, mixed_rows = run_place(slot_map, cache, gath, rows)
    return mixed_rows, new_cache.reshape(state_cache.shape)


def solution(mesh):
    return jax.shard_map(
        shards,
        mesh=mesh,
        in_specs=(
            P("seq", "head"),
            P("seq", "head"),
            P("seq", "head"),
            P("seq", "head"),
            P("seq", "head"),
            P("seq", "head"),
            P("head"),
            P("head"),
            P(),
            P(("seq", "head"), None, None, None),
        ),
        out_specs=(P("seq", "head"), P(("seq", "head"), None, None, None)),
        check_vma=False,
    )
```

```python
import functools

import jax
import jax.numpy as jnp
from jax import lax
from jax.experimental import pallas as pl
from jax.experimental.pallas import tpu as pltpu
from jax.sharding import PartitionSpec as P

MESH = pl.DeviceIdType.MESH
F32 = jnp.float32
BF16 = jnp.bfloat16

HEADS = 128
HEAD_DIM = 64
STATE = 256
GROUPS = 4
SPAN = 256
BLOCKS = 4
TOKENS = SPAN * BLOCKS
LOCAL_HEADS = 32
PAIRS = 16
CHIPS = 16
HALF = 128
ROWS = HALF + 8
WIDE = PAIRS * 128
LOG2E = 1.4426950408889634
LAG = 3
TOP = 127.9999
EARLY = 4
MIDDLE = 1
SWITCH = 3
PASS = 14
CUT_B, CUT_C = 96, 112


def dot(a, b):
    return jnp.dot(a, b, preferred_element_type=F32)


def lanes_of(p):
    return pl.ds(pl.multiple_of(p * 128, 128), 128)


ROUTE = (
    (2, 2), (1, 2), (2, 1), (3, 2), (2, 3), (1, 1), (3, 3), (1, 3), (3, 1),
    (2, 0), (0, 2), (1, 0), (0, 1), (3, 0), (0, 3), (0, 0),
)


def pick_step(i, which):
    step = ROUTE[0][which]
    for j in range(1, len(ROUTE)):
        step = jnp.where(i == j, ROUTE[j][which], step)
    return step


def mixer_kernel(
    values, gate, b_ref, c_ref, rates, steps, skip, gain, cache,
    ob, held, ga, gb, gc,
    xv, zv, adds, ins, fac, sbuf, prt, cbuf, own_in, ebuf, ent_in, mbuf, pin, entry,
    bt, ip, rcol, minus, wtop, wlow, run_t, step_t, trail_t, dwide, dec, ddec, sq, fin,
    xsem, zsem, ps_s, ps_r, os_s, os_r, en_s, en_r, ms_s, ms_r,
    gl_s, g1_s, g1_r, g2_s, g2_r, g3_s, g3_r, gh_s, gh_r, gp_s, gp_r, held_sem,
):
    seq = lax.axis_index("seq")
    y = lax.axis_index("head")
    c = seq // 2
    k = lax.rem(seq, 2)
    zc = lax.rem(c, 4)
    xc = c // 4
    partner = 2 * c + 1 - k

    def served(i):
        return lax.rem(xc + pick_step(i, 0), 4) * 4 + lax.rem(zc + pick_step(i, 1), 4)

    def serving(i):
        return lax.rem(xc + 4 - pick_step(i, 0), 4) * 4 + lax.rem(zc + 4 - pick_step(i, 1), 4)

    first = k == 0

    barrier = pltpu.get_barrier_semaphore()
    pl.semaphore_signal(barrier, inc=1, device_id={"seq": partner}, device_id_type=MESH)

    def greet(i, _):
        peer = lax.rem(c + 1 + i, CHIPS)
        pl.semaphore_signal(barrier, inc=1, device_id={"seq": 2 * peer + k}, device_id_type=MESH)
        return 0

    lax.fori_loop(0, CHIPS - 1, greet, 0)
    for j in range(1, GROUPS):
        pl.semaphore_signal(
            barrier, inc=1, device_id={"head": lax.rem(y + j, GROUPS)}, device_id_type=MESH
        )

    def x_copy(p):
        return pltpu.make_async_copy(values.at[:, lanes_of(p)], xv.at[:, lanes_of(p)], xsem.at[p])

    def start_x(i, _):
        x_copy(served(i)).start()
        return 0

    lax.fori_loop(0, PAIRS, start_x, 0)
    z_copy = pltpu.make_async_copy(gate, zv, zsem)
    z_copy.start()
    held_copy = pltpu.make_async_copy(cache, held, held_sem)
    held_copy.start()

    lane = lax.broadcasted_iota(jnp.int32, (SPAN, 128), 1)
    low = lane < 64
    upper = (
        lax.broadcasted_iota(jnp.int32, (SPAN, SPAN), 0)
        <= lax.broadcasted_iota(jnp.int32, (SPAN, SPAN), 1)
    ).astype(BF16)
    causal = (
        lax.broadcasted_iota(jnp.int32, (SPAN, SPAN), 0)
        >= lax.broadcasted_iota(jnp.int32, (SPAN, SPAN), 1)
    )
    low16 = lax.broadcasted_iota(jnp.int32, (PAIRS, 128), 1) < 64
    for b in range(BLOCKS):
        rows = slice(b * SPAN, (b + 1) * SPAN)
        run_b = dot(rates[:, rows], upper) * LOG2E
        step_b = steps[:, rows].astype(F32)
        parts, rest = [], -run_b
        for _ in range(3):
            parts.append(rest.astype(BF16).astype(F32))
            rest = rest - parts[-1]
        parts.append(jnp.zeros((128 - 3 * LOCAL_HEADS, SPAN), F32))
        rcol[rows, :] = jnp.concatenate(parts, axis=0).T.astype(BF16)
        total = run_b[:, SPAN - 1 : SPAN]
        run_t[:, rows] = run_b
        step_t[:, rows] = step_b
        trail_t[:, rows] = jnp.exp2(run_b - total) * step_b
        dwide[...] = jnp.broadcast_to(jnp.exp2(-total), (LOCAL_HEADS, 128))
        part = jnp.where(low16, dwide[pl.ds(0, PAIRS, 2), :], dwide[pl.ds(1, PAIRS, 2), :])
        dec[b] = part
        ddec[...] = part if b == 0 else ddec[...] * part
        bt[b] = b_ref[rows, :].astype(F32).T
        inner_prod = lax.dot_general(
            c_ref[rows, :], b_ref[rows, :], (((1,), (1,)), ((), ())), preferred_element_type=F32
        )
        ip[b] = jnp.where(causal, inner_prod, 0.0)

    def partner_copy(p):
        return pltpu.make_async_remote_copy(
            src_ref=sbuf.at[p, 1 - k], dst_ref=prt.at[p], send_sem=ps_s.at[p], recv_sem=ps_r.at[p],
            device_id={"seq": partner}, device_id_type=MESH,
        )

    def owner_copy(p):
        return pltpu.make_async_remote_copy(
            src_ref=cbuf.at[p], dst_ref=own_in.at[c], send_sem=os_s.at[p], recv_sem=os_r.at[c],
            device_id={"seq": 2 * p + k}, device_id_type=MESH,
        )

    def owner_arrival(j):
        return pltpu.make_async_remote_copy(
            src_ref=cbuf.at[j], dst_ref=own_in.at[j], send_sem=os_s.at[j], recv_sem=os_r.at[j],
            device_id={"seq": 2 * j + k}, device_id_type=MESH,
        )

    def states(p):
        ln = lanes_of(p)
        state = None
        for b in range(BLOCKS):
            rows = slice(b * SPAN, (b + 1) * SPAN)
            x = xv[rows, ln]
            wide = bt[b]
            s0 = (wide * trail_t[pl.ds(2 * p, 1), rows]).astype(BF16)
            s1 = (wide * trail_t[pl.ds(2 * p + 1, 1), rows]).astype(BF16)
            add = jnp.where(low, dot(s0, x), dot(s1, x))
            if b < BLOCKS - 1:
                adds[b, :, ln] = add
            state = add if b == 0 else state * dec[b, pl.ds(p, 1), :] + add
        decay = jnp.broadcast_to(ddec[pl.ds(p, 1), :], (8, 128))
        for h in range(2):
            sbuf[p, h, 0:HALF, :] = state[h * HALF : (h + 1) * HALF]
            sbuf[p, h, HALF:ROWS, :] = decay

    def combine(p):
        partner_copy(p).wait_recv()
        here = sbuf[p, k]
        there = prt[p]
        early = jnp.where(first, here, there)
        late = jnp.where(first, there, here)
        decay = late[HALF : HALF + 1, :]
        return early[0:HALF] * decay + late[0:HALF], early[HALF:ROWS] * late[HALF:ROWS]

    def send_owner(p):
        both, decay = combine(p)
        cbuf[p, 0:HALF, :] = both
        cbuf[p, HALF:ROWS, :] = decay
        owner_copy(p).start()

    def states_step(i, _):
        first_p, second_p = served(2 * i), served(2 * i + 1)
        x_copy(first_p).wait()
        x_copy(second_p).wait()
        states(first_p)
        states(second_p)

        @pl.when(i == 0)
        def _():
            pl.semaphore_wait(barrier, 1 + (CHIPS - 1) + (GROUPS - 1))

        partner_copy(first_p).start()
        partner_copy(second_p).start()

        @pl.when(i >= 1)
        def _():
            send_owner(served(2 * i - 2))
            send_owner(served(2 * i - 1))

        return 0

    lax.fori_loop(0, PAIRS // 2, states_step, 0)
    send_owner(served(PAIRS - 2))
    both, decay = combine(c)
    own_in[c, 0:HALF, :] = both
    own_in[c, HALF:ROWS, :] = decay

    row_s = lax.rem(lax.broadcasted_iota(jnp.int32, (128, 256), 0), LOCAL_HEADS)
    lane_s = lax.broadcasted_iota(jnp.int32, (128, 256), 1) // 128
    head_s = row_s - lane_s

    def spread(p, slot):
        pick = jnp.where(head_s == 2 * p, 1.0, 0.0).astype(BF16)
        for b in range(BLOCKS):
            rows = slice(b * SPAN, (b + 1) * SPAN)
            minus[slot, rows, :] = dot(rcol[rows, :], pick)

    def weigh(p, slot, b):
        ln = lanes_of(p)
        r0 = b * SPAN
        rows = slice(r0, r0 + SPAN)
        m = [minus[slot, rows, 128 * h : 128 * h + 128] for h in range(2)]
        fac[rows, ln] = jnp.exp2(jnp.where(low, m[0], m[1]))
        for h in range(2):
            ru = run_t[pl.ds(2 * p + h, 1), rows]
            st = step_t[pl.ds(2 * p + h, 1), rows]
            near = slice(128 * h, 128 * h + 128)
            w00 = jnp.exp2(jnp.minimum(ru[:, :128] + m[h][:128], TOP)) * ip[b, :128, :128] * st[:, :128]
            wtop[slot, b, near, :] = w00.astype(BF16)
            w10 = jnp.exp2(ru[:, :128] + m[h][128:]) * ip[b, 128:, :128] * st[:, :128]
            wlow[slot, b, near, 0:128] = w10.astype(BF16)
            w11 = jnp.exp2(jnp.minimum(ru[:, 128:] + m[h][128:], TOP)) * ip[b, 128:, 128:] * st[:, 128:]
            wlow[slot, b, near, 128:256] = w11.astype(BF16)

    def apply(p, slot, b):
        ln = lanes_of(p)
        r0 = b * SPAN
        x = xv[r0 : r0 + SPAN, ln]
        top = dot(wtop[slot, b], x[:128])
        bottom = dot(wlow[slot, b], x)
        ins[r0 : r0 + 128, ln] = jnp.where(low[:128], top[:128], top[128:])
        ins[r0 + 128 : r0 + 256, ln] = jnp.where(low[:128], bottom[:128], bottom[128:])

    def inner(i, _):
        p0, p1 = 2 * i, 2 * i + 1
        old = lax.rem(p1 + PAIRS - 2, PAIRS)
        for b in range(BLOCKS):
            apply(old, 1, b)
            weigh(p0, 0, b)
        spread(lax.rem(p0 + 2, PAIRS), 0)
        for b in range(BLOCKS):
            apply(p0, 0, b)
            weigh(p1, 1, b)
        spread(lax.rem(p1 + 2, PAIRS), 1)
        return 0

    wtop[1] = jnp.zeros_like(wtop[1])
    wlow[1] = jnp.zeros_like(wlow[1])
    spread(0, 0)
    spread(1, 1)
    lax.fori_loop(0, EARLY, inner, 0)

    def scan_step(j, state):
        @pl.when(j != c)
        def _():
            owner_arrival(j).wait_recv()

        ebuf[j] = state
        return state * own_in[j, HALF : HALF + 1, :] + own_in[j, 0:HALF, :]

    last = lax.fori_loop(0, CHIPS, scan_step, jnp.zeros((HALF, 128), F32))
    fin[...] = last.T.astype(BF16)

    rows_a, rows_b, rows_c = pl.ds(0, CUT_B), pl.ds(CUT_B, CUT_C - CUT_B), pl.ds(CUT_C, 128 - CUT_C)
    parts = ((rows_a, ga, "zxy"), (rows_b, gb, "yzx"), (rows_c, gc, "yxz"))

    def keep(n):
        rows, g, _ = parts[n]
        return pltpu.make_async_copy(fin.at[rows], g.at[k, y, xc, zc], gl_s.at[n])

    def peer(axis, j):
        if axis == "y":
            return {"head": lax.rem(y + j, 4)}
        if axis == "x":
            return {"seq": 2 * (lax.rem(xc + j, 4) * 4 + zc) + k}
        return {"seq": 2 * (xc * 4 + lax.rem(zc + j, 4)) + k}

    def region(g, done, axis, j):
        at = {"y": y, "x": xc, "z": zc}
        if j:
            at[axis] = lax.rem(at[axis] + 4 - j, 4)
        index = [k] + [slice(None) if a in done else at[a] for a in "yxz"]
        return g.at[tuple(index)]

    def stage_copy(n, stage, j, arrival):
        rows, g, order = parts[n]
        axis = order[stage]
        there = region(g, order[:stage], axis, j if arrival else 0)
        source = fin.at[rows] if stage == 0 else there
        sem_s, sem_r = ((g1_s, g1_r), (g2_s, g2_r), (g3_s, g3_r))[stage]
        return pltpu.make_async_remote_copy(
            src_ref=source, dst_ref=there, send_sem=sem_s.at[n, j - 1], recv_sem=sem_r.at[n, j - 1],
            device_id=peer(axis, j), device_id_type=MESH,
        )

    def stage_send(n, stage):
        for j in (1, 3, 2):
            stage_copy(n, stage, j, False).start()

    def stage_arrive(n, stage):
        for j in (1, 3, 2):
            stage_copy(n, stage, j, True).wait_recv()

    def pass_on(j, arrival):
        half = pl.ds(0, 2) if j == 1 else pl.ds(2, 2)
        at = lax.rem(y + (2 if arrival else 4 - j), 4)
        part = ga.at[k, at, half]
        return pltpu.make_async_remote_copy(
            src_ref=part, dst_ref=part, send_sem=gh_s.at[j // 2], recv_sem=gh_r.at[j // 2],
            device_id=peer("y", j), device_id_type=MESH,
        )

    for n in range(3):
        keep(n).start()
    for n in range(3):
        stage_send(n, 0)

    def entry_copy(j):
        return pltpu.make_async_remote_copy(
            src_ref=ebuf.at[j], dst_ref=ent_in.at[c], send_sem=en_s.at[j], recv_sem=en_r.at[c],
            device_id={"seq": 2 * j + k}, device_id_type=MESH,
        )

    def entry_arrival(p):
        return pltpu.make_async_remote_copy(
            src_ref=ebuf.at[p], dst_ref=ent_in.at[p], send_sem=en_s.at[p], recv_sem=en_r.at[p],
            device_id={"seq": 2 * p + k}, device_id_type=MESH,
        )

    def send_entry(i, _):
        entry_copy(served(i)).start()
        return 0

    lax.fori_loop(EARLY, EARLY + MIDDLE, inner, 0)
    for n in range(3):
        keep(n).wait()
        stage_arrive(n, 0)
        stage_send(n, 1)
    lax.fori_loop(0, CHIPS - 1, send_entry, 0)
    ent_in[c] = ebuf[c]

    lax.fori_loop(EARLY + MIDDLE, PAIRS // 2, inner, 0)
    for b in range(BLOCKS):
        apply(PAIRS - 1, 1, b)

    def entry_to_partner(p):
        return pltpu.make_async_remote_copy(
            src_ref=mbuf.at[p], dst_ref=pin.at[p], send_sem=ms_s.at[p], recv_sem=ms_r.at[p],
            device_id={"seq": partner}, device_id_type=MESH,
        )

    z_copy.wait()
    sq[...] = jnp.zeros_like(sq)

    def receive(p):
        @pl.when(p != c)
        def _():
            entry_arrival(p).wait_recv()

        state = ent_in[p]
        early = jnp.where(first, sbuf[p, 0], prt[p])
        moved = state * early[HALF : HALF + 1, :] + early[0:HALF]
        entry[pl.ds(pl.multiple_of(k * HALF, HALF), HALF), lanes_of(p)] = jnp.where(first, state, moved)
        mbuf[p] = jnp.where(first, moved, state)
        entry_to_partner(p).start()

    def finish(p):
        ln = lanes_of(p)
        entry_to_partner(p).wait_recv()
        entry[pl.ds(pl.multiple_of((1 - k) * HALF, HALF), HALF), ln] = pin[p]
        state = entry[:, ln]
        skip_row = jnp.where(low[0:1], skip[2 * p], skip[2 * p + 1])
        for b in range(BLOCKS):
            rows = slice(b * SPAN, (b + 1) * SPAN)
            carried = dot(c_ref[rows, :], state.astype(BF16))
            ssd = (ins[rows, ln] + carried * fac[rows, ln]).astype(BF16).astype(F32)
            z = zv[rows, ln].astype(F32)
            half_z = z * 0.5
            gated = (ssd + xv[rows, ln].astype(F32) * skip_row) * (half_z + half_z * jnp.tanh(half_z))
            ins[rows, ln] = gated
            sq[rows, :] = sq[rows, :] + gated * gated
            if b < BLOCKS - 1:
                state = state * dec[b, pl.ds(p, 1), :] + adds[b, :, ln]

    def finish_step(i, _):
        @pl.when(i < PAIRS)
        def _():
            receive(serving(lax.rem(i + PAIRS - 1, PAIRS)))

        @pl.when(i >= LAG)
        def _():
            finish(serving(lax.rem(i + PAIRS - 1 - LAG, PAIRS)))

        return 0

    def to_partner(n, at, half):
        g = parts[n][1]
        if n == 0:
            return g.at[half, at]
        return g.at[half]

    def p_copy(i, arrival):
        n = 0 if i < 4 else i - 3
        at = lax.rem(y + 4 - i, 4)
        part = to_partner(n, at, 1 - k if arrival else k)
        return pltpu.make_async_remote_copy(
            src_ref=part, dst_ref=part, send_sem=gp_s.at[i], recv_sem=gp_r.at[i],
            device_id={"seq": partner}, device_id_type=MESH,
        )

    lax.fori_loop(0, SWITCH, finish_step, 0)
    stage_arrive(0, 1)
    for j in (1, 3):
        stage_copy(0, 2, j, False).start()
    for n in (1, 2):
        stage_arrive(n, 1)
        stage_send(n, 2)
    p_copy(0, False).start()
    lax.fori_loop(SWITCH, PASS, finish_step, 0)
    for j in (1, 3):
        stage_copy(0, 2, j, True).wait_recv()
        pass_on(j, False).start()
        p_copy(j, False).start()
    lax.fori_loop(PASS, PAIRS + LAG, finish_step, 0)

    for b in range(BLOCKS):
        rows = slice(b * SPAN, (b + 1) * SPAN)
        mean = jnp.sum(sq[rows, :], axis=1, keepdims=True) * (1.0 / WIDE)
        inverse = jnp.broadcast_to(lax.rsqrt(mean + 1e-05), (SPAN, 128))

        def norm_step(p, _, rows=rows, inverse=inverse):
            ln = lanes_of(p)
            ob[rows, ln] = (ins[rows, ln] * inverse * gain[pl.ds(p, 1), :]).astype(BF16)
            return 0

        lax.fori_loop(0, PAIRS, norm_step, 0)

    for n in (1, 2):
        stage_arrive(n, 2)
        p_copy(3 + n, False).start()
    for j in (1, 3):
        pass_on(j, True).wait_recv()
    p_copy(2, False).start()
    held_copy.wait()
    for n in range(3):
        for stage in range(3):
            for j in (1, 3) if (n, stage) == (0, 2) else (1, 2, 3):
                stage_copy(n, stage, j, False).wait_send()
    for j in (1, 3):
        pass_on(j, False).wait_send()
    for i in range(6):
        p_copy(i, False).wait_send()
        p_copy(i, True).wait_recv()

    def drain(p, _):
        partner_copy(p).wait_send()
        entry_to_partner(p).wait_send()

        @pl.when(p != c)
        def _():
            owner_copy(p).wait_send()
            entry_copy(p).wait_send()

        return 0

    lax.fori_loop(0, PAIRS, drain, 0)


def run_mixer(values, gate, input_map, output_map, rates, steps, skip, gain, cache):
    vm = lambda *shape: pltpu.VMEM(shape, F32)
    dma = lambda *shape: pltpu.SemaphoreType.DMA(shape)
    any_spec = pl.BlockSpec(memory_space=pl.ANY)
    vmem_spec = pl.BlockSpec(memory_space=pltpu.VMEM)
    return pl.pallas_call(
        mixer_kernel,
        out_shape=(
            pltpu.VMEM((TOKENS, WIDE), BF16),
            pltpu.VMEM((GROUPS, 4, 4, 128, STATE), BF16),
            jax.ShapeDtypeStruct((2, GROUPS, 4, 4, CUT_B, HALF), BF16),
            jax.ShapeDtypeStruct((2, GROUPS, 4, 4, CUT_C - CUT_B, HALF), BF16),
            jax.ShapeDtypeStruct((2, GROUPS, 4, 4, 128 - CUT_C, HALF), BF16),
        ),
        in_specs=[any_spec, any_spec] + [vmem_spec] * 4 + [pl.BlockSpec(memory_space=pltpu.SMEM), vmem_spec, any_spec],
        out_specs=(vmem_spec, vmem_spec) + (any_spec,) * 3,
        scratch_shapes=[
            pltpu.VMEM((TOKENS, WIDE), BF16),
            pltpu.VMEM((TOKENS, WIDE), BF16),
            vm(BLOCKS - 1, STATE, WIDE),
            vm(TOKENS, WIDE),
            vm(TOKENS, WIDE),
            vm(PAIRS, 2, ROWS, 128),
            vm(PAIRS, ROWS, 128),
            vm(PAIRS, ROWS, 128),
            vm(CHIPS, ROWS, 128),
            vm(CHIPS, HALF, 128),
            vm(PAIRS, HALF, 128),
            vm(PAIRS, HALF, 128),
            vm(PAIRS, HALF, 128),
            vm(STATE, WIDE),
            vm(BLOCKS, STATE, SPAN),
            vm(BLOCKS, SPAN, SPAN),
            pltpu.VMEM((TOKENS, 128), BF16),
            vm(2, TOKENS, 256),
            pltpu.VMEM((2, BLOCKS, 256, 128), BF16),
            pltpu.VMEM((2, BLOCKS, 256, 256), BF16),
            vm(LOCAL_HEADS, TOKENS),
            vm(LOCAL_HEADS, TOKENS),
            vm(LOCAL_HEADS, TOKENS),
            vm(LOCAL_HEADS, 128),
            vm(BLOCKS, PAIRS, 128),
            vm(PAIRS, 128),
            vm(TOKENS, 128),
            pltpu.VMEM((128, HALF), BF16),
            dma(PAIRS), pltpu.SemaphoreType.DMA,
            dma(PAIRS), dma(PAIRS),
            dma(PAIRS), dma(PAIRS),
            dma(PAIRS), dma(PAIRS),
            dma(PAIRS), dma(PAIRS),
            dma(3),
            dma(3, 3), dma(3, 3), dma(3, 3), dma(3, 3), dma(3, 3), dma(3, 3), dma(2), dma(2), dma(6), dma(6),
            pltpu.SemaphoreType.DMA,
        ],
        compiler_params=pltpu.CompilerParams(
            collective_id=0, has_side_effects=True, vmem_limit_bytes=54 * 1024 * 1024
        ),
        cost_estimate=pl.CostEstimate(flops=6_000_000_000, bytes_accessed=24_000_000, transcendentals=12_000_000),
        name="mixer",
    )(values, gate, input_map, output_map, rates, steps, skip, gain, cache)


def place_kernel(slot_map, held, rows_in, ga, gb, gc, out, rows_out, buf, hin, cout, rout):
    rank = lax.axis_index("seq") * GROUPS + lax.axis_index("head")

    def final_in(g):
        for h in range(2):
            for n, (part, start, stop) in enumerate(
                ((ga, 0, CUT_B), (gb, CUT_B, CUT_C), (gc, CUT_C, 128))
            ):
                yield pltpu.make_async_copy(
                    part.at[h, g],
                    buf.at[g, :, :, pl.ds(start, stop - start), pl.ds(h * HALF, HALF)],
                    hin.at[g, 3 * h + n],
                )

    def rows_copy(b):
        rows = pl.ds(b * SPAN, SPAN)
        return pltpu.make_async_copy(rows_in.at[rows], rows_out.at[rows], rout.at[b])

    for g in range(GROUPS):
        hit = slot_map[g] == rank

        @pl.when(hit)
        def _(g=g):
            for copy in final_in(g):
                copy.start()

        @pl.when(jnp.logical_not(hit))
        def _(g=g):
            pltpu.make_async_copy(held.at[g], out.at[g], cout.at[g]).start()

        rows_copy(g).start()

    for g in range(GROUPS):
        hit = slot_map[g] == rank

        @pl.when(hit)
        def _(g=g):
            for copy in final_in(g):
                copy.wait()
            pltpu.make_async_copy(buf.at[g], out.at[g], cout.at[g]).start()

    for g in range(GROUPS):
        pltpu.make_async_copy(held.at[g], out.at[g], cout.at[g]).wait()
        rows_copy(g).wait()


def run_place(slot_map, held, rows, ga, gb, gc):
    any_spec = pl.BlockSpec(memory_space=pl.ANY)
    vmem_spec = pl.BlockSpec(memory_space=pltpu.VMEM)
    return pl.pallas_call(
        place_kernel,
        out_shape=(
            jax.ShapeDtypeStruct((GROUPS, 4, 4, 128, STATE), BF16),
            jax.ShapeDtypeStruct((TOKENS, WIDE), BF16),
        ),
        in_specs=[pl.BlockSpec(memory_space=pltpu.SMEM), vmem_spec, vmem_spec] + [any_spec] * 3,
        out_specs=(any_spec, any_spec),
        scratch_shapes=[
            pltpu.VMEM((GROUPS, 4, 4, 128, STATE), BF16),
            pltpu.SemaphoreType.DMA((GROUPS, 6)),
            pltpu.SemaphoreType.DMA((GROUPS,)),
            pltpu.SemaphoreType.DMA((GROUPS,)),
        ],
        compiler_params=pltpu.CompilerParams(vmem_limit_bytes=16 * 1024 * 1024),
        name="place",
    )(slot_map, held, rows, ga, gb, gc)


def shards(
    values, gate_rows, input_map, output_map, decay_rate, step_size, skip_gain, norm_gain, slot_map, state_cache
):
    gain = norm_gain.reshape(PAIRS, 128)
    cache = state_cache.reshape(GROUPS, 4, 4, 128, STATE)
    rows, held, ga, gb, gc = run_mixer(
        values, gate_rows, input_map, output_map, decay_rate.T, step_size.T, skip_gain, gain, cache
    )
    held, rows = (pltpu.with_memory_space_constraint(a, pltpu.VMEM) for a in (held, rows))
    ga, gb, gc = (pltpu.with_memory_space_constraint(a, pltpu.HBM) for a in (ga, gb, gc))
    new_cache, mixed_rows = run_place(slot_map, held, rows, ga, gb, gc)
    return mixed_rows, new_cache.reshape(state_cache.shape)


def solution(mesh):
    return jax.shard_map(
        shards,
        mesh=mesh,
        in_specs=(
            P("seq", "head"),
            P("seq", "head"),
            P("seq", "head"),
            P("seq", "head"),
            P("seq", "head"),
            P("seq", "head"),
            P("head"),
            P("head"),
            P(),
            P(("seq", "head"), None, None, None),
        ),
        out_specs=(P("seq", "head"), P(("seq", "head"), None, None, None)),
        check_vma=False,
    )
```

```python
import functools

import jax
import jax.numpy as jnp
from jax import lax
from jax.experimental import pallas as pl
from jax.experimental.pallas import tpu as pltpu
from jax.sharding import PartitionSpec as P

MESH = pl.DeviceIdType.MESH
F32 = jnp.float32
BF16 = jnp.bfloat16

HEADS = 128
HEAD_DIM = 64
STATE = 256
GROUPS = 4
SPAN = 256
BLOCKS = 4
TOKENS = SPAN * BLOCKS
LOCAL_HEADS = 32
PAIRS = 16
CHIPS = 16
HALF = 128
ROWS = HALF + 8
WIDE = PAIRS * 128
LOG2E = 1.4426950408889634
LAG = 3
TOP = 127.9999
EARLY = 7
AHEAD = 6
MIDDLE = 1
SWITCH = 3
PASS = 5
CUT_B, CUT_C = 96, 112


def dot(a, b):
    return jnp.dot(a, b, preferred_element_type=F32)


def lanes_of(p):
    return pl.ds(pl.multiple_of(p * 128, 128), 128)


ROUTE = (
    (2, 2), (1, 2), (2, 1), (3, 2), (2, 3), (1, 1), (3, 3), (1, 3), (3, 1),
    (2, 0), (0, 2), (1, 0), (0, 1), (3, 0), (0, 3), (0, 0),
)


def pick_step(i, which):
    step = ROUTE[0][which]
    for j in range(1, len(ROUTE)):
        step = jnp.where(i == j, ROUTE[j][which], step)
    return step


def mixer_kernel(
    values, gate, b_ref, c_ref, rates, steps, skip, gain, cache,
    ob, held, ga, gb, gc,
    xv, zv, adds, ins, fac, sbuf, prt, cbuf, own_in, ebuf, ent_in, mbuf, pin, entry,
    bt, ip, rcol, minus, wtop, wlow, run_t, step_t, trail_t, dwide, dec, ddec, sq, fin,
    xsem, zsem, ps_s, ps_r, os_s, os_r, en_s, en_r, ms_s, ms_r,
    gl_s, g1_s, g1_r, g2_s, g2_r, g3_s, g3_r, gy_s, gy_r, gd_s, gd_r, gp_s, gp_r, held_sem,
):
    seq = lax.axis_index("seq")
    y = lax.axis_index("head")
    c = seq // 2
    k = lax.rem(seq, 2)
    zc = lax.rem(c, 4)
    xc = c // 4
    partner = 2 * c + 1 - k

    def served(i):
        return lax.rem(xc + pick_step(i, 0), 4) * 4 + lax.rem(zc + pick_step(i, 1), 4)

    def serving(i):
        return lax.rem(xc + 4 - pick_step(i, 0), 4) * 4 + lax.rem(zc + 4 - pick_step(i, 1), 4)

    first = k == 0

    def x_copy(p):
        return pltpu.make_async_copy(values.at[:, lanes_of(p)], xv.at[:, lanes_of(p)], xsem.at[p])

    def start_x(i, _):
        x_copy(served(i)).start()
        return 0

    lax.fori_loop(0, PAIRS, start_x, 0)
    barrier = pltpu.get_barrier_semaphore()
    pl.semaphore_signal(barrier, inc=1, device_id={"seq": partner}, device_id_type=MESH)

    def greet(i, _):
        peer = lax.rem(c + 1 + i, CHIPS)
        pl.semaphore_signal(barrier, inc=1, device_id={"seq": 2 * peer + k}, device_id_type=MESH)
        return 0

    lax.fori_loop(0, CHIPS - 1, greet, 0)
    for j in range(1, GROUPS):
        pl.semaphore_signal(
            barrier, inc=1, device_id={"head": lax.rem(y + j, GROUPS)}, device_id_type=MESH
        )

    z_copy = pltpu.make_async_copy(gate, zv, zsem)
    held_copy = pltpu.make_async_copy(cache, held, held_sem)

    lane = lax.broadcasted_iota(jnp.int32, (SPAN, 128), 1)
    low = lane < 64
    upper = (
        lax.broadcasted_iota(jnp.int32, (SPAN, SPAN), 0)
        <= lax.broadcasted_iota(jnp.int32, (SPAN, SPAN), 1)
    ).astype(BF16)
    causal = (
        lax.broadcasted_iota(jnp.int32, (SPAN, SPAN), 0)
        >= lax.broadcasted_iota(jnp.int32, (SPAN, SPAN), 1)
    )
    low16 = lax.broadcasted_iota(jnp.int32, (PAIRS, 128), 1) < 64
    for b in range(BLOCKS):
        rows = slice(b * SPAN, (b + 1) * SPAN)
        run_b = dot(rates[:, rows], upper) * LOG2E
        step_b = steps[:, rows].astype(F32)
        parts, rest = [], -run_b
        for _ in range(3):
            parts.append(rest.astype(BF16).astype(F32))
            rest = rest - parts[-1]
        parts.append(jnp.zeros((128 - 3 * LOCAL_HEADS, SPAN), F32))
        rcol[rows, :] = jnp.concatenate(parts, axis=0).T.astype(BF16)
        total = run_b[:, SPAN - 1 : SPAN]
        run_t[:, rows] = run_b
        step_t[:, rows] = step_b
        trail_t[:, rows] = jnp.exp2(run_b - total) * step_b
        dwide[...] = jnp.broadcast_to(jnp.exp2(-total), (LOCAL_HEADS, 128))
        part = jnp.where(low16, dwide[pl.ds(0, PAIRS, 2), :], dwide[pl.ds(1, PAIRS, 2), :])
        dec[b] = part
        ddec[...] = part if b == 0 else ddec[...] * part
        bt[b] = b_ref[rows, :].astype(F32).T
        inner_prod = lax.dot_general(
            c_ref[rows, :], b_ref[rows, :], (((1,), (1,)), ((), ())), preferred_element_type=F32
        )
        ip[b] = jnp.where(causal, inner_prod, 0.0)

    def partner_copy(p):
        return pltpu.make_async_remote_copy(
            src_ref=sbuf.at[p, 1 - k], dst_ref=prt.at[p], send_sem=ps_s.at[p], recv_sem=ps_r.at[p],
            device_id={"seq": partner}, device_id_type=MESH,
        )

    def owner_copy(p):
        return pltpu.make_async_remote_copy(
            src_ref=cbuf.at[p], dst_ref=own_in.at[c], send_sem=os_s.at[p], recv_sem=os_r.at[c],
            device_id={"seq": 2 * p + k}, device_id_type=MESH,
        )

    def owner_arrival(j):
        return pltpu.make_async_remote_copy(
            src_ref=cbuf.at[j], dst_ref=own_in.at[j], send_sem=os_s.at[j], recv_sem=os_r.at[j],
            device_id={"seq": 2 * j + k}, device_id_type=MESH,
        )

    def states(p):
        ln = lanes_of(p)
        state = None
        for b in range(BLOCKS):
            rows = slice(b * SPAN, (b + 1) * SPAN)
            x = xv[rows, ln]
            wide = bt[b]
            s0 = (wide * trail_t[pl.ds(2 * p, 1), rows]).astype(BF16)
            s1 = (wide * trail_t[pl.ds(2 * p + 1, 1), rows]).astype(BF16)
            add = jnp.where(low, dot(s0, x), dot(s1, x))
            if b < BLOCKS - 1:
                adds[b, :, ln] = add
            state = add if b == 0 else state * dec[b, pl.ds(p, 1), :] + add
        decay = jnp.broadcast_to(ddec[pl.ds(p, 1), :], (8, 128))
        for h in range(2):
            sbuf[p, h, 0:HALF, :] = state[h * HALF : (h + 1) * HALF]
            sbuf[p, h, HALF:ROWS, :] = decay

    def combine(p):
        partner_copy(p).wait_recv()
        here = sbuf[p, k]
        there = prt[p]
        early = jnp.where(first, here, there)
        late = jnp.where(first, there, here)
        decay = late[HALF : HALF + 1, :]
        return early[0:HALF] * decay + late[0:HALF], early[HALF:ROWS] * late[HALF:ROWS]

    def send_owner(p):
        both, decay = combine(p)
        cbuf[p, 0:HALF, :] = both
        cbuf[p, HALF:ROWS, :] = decay
        owner_copy(p).start()

    def states_step(i, _):
        first_p, second_p = served(2 * i), served(2 * i + 1)
        x_copy(first_p).wait()
        x_copy(second_p).wait()
        states(first_p)
        states(second_p)

        @pl.when(i == 0)
        def _():
            pl.semaphore_wait(barrier, 1 + (CHIPS - 1) + (GROUPS - 1))

        partner_copy(first_p).start()
        partner_copy(second_p).start()

        @pl.when(i >= 1)
        def _():
            send_owner(served(2 * i - 2))
            send_owner(served(2 * i - 1))

        return 0

    lax.fori_loop(0, PAIRS // 2, states_step, 0)
    z_copy.start()
    held_copy.start()
    send_owner(served(PAIRS - 2))
    both, decay = combine(c)
    own_in[c, 0:HALF, :] = both
    own_in[c, HALF:ROWS, :] = decay

    row_s = lax.rem(lax.broadcasted_iota(jnp.int32, (128, 256), 0), LOCAL_HEADS)
    lane_s = lax.broadcasted_iota(jnp.int32, (128, 256), 1) // 128
    head_s = row_s - lane_s

    def spread(p, slot):
        pick = jnp.where(head_s == 2 * p, 1.0, 0.0).astype(BF16)
        for b in range(BLOCKS):
            rows = slice(b * SPAN, (b + 1) * SPAN)
            minus[slot, rows, :] = dot(rcol[rows, :], pick)

    def weigh(p, slot, b):
        ln = lanes_of(p)
        r0 = b * SPAN
        rows = slice(r0, r0 + SPAN)
        m = [minus[slot, rows, 128 * h : 128 * h + 128] for h in range(2)]
        fac[rows, ln] = jnp.exp2(jnp.where(low, m[0], m[1]))
        for h in range(2):
            ru = run_t[pl.ds(2 * p + h, 1), rows]
            st = step_t[pl.ds(2 * p + h, 1), rows]
            near = slice(128 * h, 128 * h + 128)
            w00 = jnp.exp2(jnp.minimum(ru[:, :128] + m[h][:128], TOP)) * ip[b, :128, :128] * st[:, :128]
            wtop[slot, b, near, :] = w00.astype(BF16)
            w10 = jnp.exp2(ru[:, :128] + m[h][128:]) * ip[b, 128:, :128] * st[:, :128]
            wlow[slot, b, near, 0:128] = w10.astype(BF16)
            w11 = jnp.exp2(jnp.minimum(ru[:, 128:] + m[h][128:], TOP)) * ip[b, 128:, 128:] * st[:, 128:]
            wlow[slot, b, near, 128:256] = w11.astype(BF16)

    def apply(p, slot, b):
        ln = lanes_of(p)
        r0 = b * SPAN
        x = xv[r0 : r0 + SPAN, ln]
        top = dot(wtop[slot, b], x[:128])
        bottom = dot(wlow[slot, b], x)
        ins[r0 : r0 + 128, ln] = jnp.where(low[:128], top[:128], top[128:])
        ins[r0 + 128 : r0 + 256, ln] = jnp.where(low[:128], bottom[:128], bottom[128:])

    def inner(i, _):
        p0, p1 = 2 * i, 2 * i + 1
        old = lax.rem(p1 + PAIRS - 2, PAIRS)
        for b in range(BLOCKS):
            apply(old, 1, b)
            weigh(p0, 0, b)
        spread(lax.rem(p0 + 2, PAIRS), 0)
        for b in range(BLOCKS):
            apply(p0, 0, b)
            weigh(p1, 1, b)
        spread(lax.rem(p1 + 2, PAIRS), 1)
        return 0

    wtop[1] = jnp.zeros_like(wtop[1])
    wlow[1] = jnp.zeros_like(wlow[1])
    spread(0, 0)
    spread(1, 1)
    lax.fori_loop(0, EARLY, inner, 0)

    def scan_step(j, state):
        @pl.when(j != c)
        def _():
            owner_arrival(j).wait_recv()

        ebuf[j] = state
        return state * own_in[j, HALF : HALF + 1, :] + own_in[j, 0:HALF, :]

    last = lax.fori_loop(0, CHIPS, scan_step, jnp.zeros((HALF, 128), F32))
    fin[...] = last.T.astype(BF16)

    rows_a, rows_b, rows_c = pl.ds(0, CUT_B), pl.ds(CUT_B, CUT_C - CUT_B), pl.ds(CUT_C, 128 - CUT_C)
    parts = ((rows_a, ga, "xzy"), (rows_b, gb, "yzx"), (rows_c, gc, "yxz"))

    def keep(n):
        rows, g, _ = parts[n]
        return pltpu.make_async_copy(fin.at[rows], g.at[k, y, xc, zc], gl_s.at[n])

    def peer(axis, j):
        if axis == "y":
            return {"head": lax.rem(y + j, 4)}
        if axis == "x":
            return {"seq": 2 * (lax.rem(xc + j, 4) * 4 + zc) + k}
        return {"seq": 2 * (xc * 4 + lax.rem(zc + j, 4)) + k}

    def region(g, done, axis, j):
        at = {"y": y, "x": xc, "z": zc}
        if j:
            at[axis] = lax.rem(at[axis] + 4 - j, 4)
        index = [k] + [slice(None) if a in done else at[a] for a in "yxz"]
        return g.at[tuple(index)]

    def stage_copy(n, stage, j, arrival):
        rows, g, order = parts[n]
        axis = order[stage]
        there = region(g, order[:stage], axis, j if arrival else 0)
        source = fin.at[rows] if stage == 0 else there
        sem_s, sem_r = ((g1_s, g1_r), (g2_s, g2_r), (g3_s, g3_r))[stage]
        return pltpu.make_async_remote_copy(
            src_ref=source, dst_ref=there, send_sem=sem_s.at[n, j - 1], recv_sem=sem_r.at[n, j - 1],
            device_id=peer(axis, j), device_id_type=MESH,
        )

    def stage_send(n, stage):
        for j in (1, 3, 2):
            stage_copy(n, stage, j, False).start()

    def stage_arrive(n, stage):
        for j in (1, 3, 2):
            stage_copy(n, stage, j, True).wait_recv()

    def y_copy(r, j, arrival):
        there = ga.at[k, lax.rem(y + 4 - j, 4) if arrival else y, lax.rem(xc + 4 - r, 4)]
        return pltpu.make_async_remote_copy(
            src_ref=there, dst_ref=there, send_sem=gy_s.at[r, j - 1], recv_sem=gy_r.at[r, j - 1],
            device_id=peer("y", j), device_id_type=MESH,
        )

    def plane_copy(d):
        return pltpu.make_async_remote_copy(
            src_ref=fin.at[rows_a], dst_ref=ga.at[k, y, xc, zc], send_sem=gd_s.at[d], recv_sem=gd_r.at[c],
            device_id={"seq": 2 * d + k}, device_id_type=MESH,
        )

    def plane_arrival(d):
        return pltpu.make_async_remote_copy(
            src_ref=fin.at[rows_a], dst_ref=ga.at[k, y, d // 4, lax.rem(d, 4)],
            send_sem=gd_s.at[d], recv_sem=gd_r.at[d],
            device_id={"seq": 2 * d + k}, device_id_type=MESH,
        )

    def plane_send(i, _):
        plane_copy(served(i)).start()
        return 0

    def row_arrive(r):
        def step(i, _):
            d = lax.rem(xc + 4 - r, 4) * 4 + i

            @pl.when(d != c)
            def _():
                plane_arrival(d).wait_recv()

            return 0

        lax.fori_loop(0, 4, step, 0)

    def y_send(r):
        for j in (1, 3, 2):
            y_copy(r, j, False).start()

    for n in range(3):
        keep(n).start()
    for n in (1, 2):
        stage_send(n, 0)
    lax.fori_loop(0, CHIPS - 1, plane_send, 0)

    def entry_copy(j):
        return pltpu.make_async_remote_copy(
            src_ref=ebuf.at[j], dst_ref=ent_in.at[c], send_sem=en_s.at[j], recv_sem=en_r.at[c],
            device_id={"seq": 2 * j + k}, device_id_type=MESH,
        )

    def entry_arrival(p):
        return pltpu.make_async_remote_copy(
            src_ref=ebuf.at[p], dst_ref=ent_in.at[p], send_sem=en_s.at[p], recv_sem=en_r.at[p],
            device_id={"seq": 2 * p + k}, device_id_type=MESH,
        )

    def send_entry(i, _):
        entry_copy(served(i)).start()
        return 0

    lax.fori_loop(0, AHEAD, send_entry, 0)
    lax.fori_loop(EARLY, EARLY + MIDDLE, inner, 0)
    for n in range(3):
        keep(n).wait()
    for n in (1, 2):
        stage_arrive(n, 0)
        stage_send(n, 1)
    row_arrive(0)
    y_send(0)
    ent_in[c] = ebuf[c]

    lax.fori_loop(EARLY + MIDDLE, PAIRS // 2, inner, 0)
    for b in range(BLOCKS):
        apply(PAIRS - 1, 1, b)

    def entry_to_partner(p):
        return pltpu.make_async_remote_copy(
            src_ref=mbuf.at[p], dst_ref=pin.at[p], send_sem=ms_s.at[p], recv_sem=ms_r.at[p],
            device_id={"seq": partner}, device_id_type=MESH,
        )

    z_copy.wait()
    sq[...] = jnp.zeros_like(sq)

    def receive(p):
        @pl.when(p != c)
        def _():
            entry_arrival(p).wait_recv()

        state = ent_in[p]
        early = jnp.where(first, sbuf[p, 0], prt[p])
        moved = state * early[HALF : HALF + 1, :] + early[0:HALF]
        entry[pl.ds(pl.multiple_of(k * HALF, HALF), HALF), lanes_of(p)] = jnp.where(first, state, moved)
        mbuf[p] = jnp.where(first, moved, state)
        entry_to_partner(p).start()

    def finish(p):
        ln = lanes_of(p)
        entry_to_partner(p).wait_recv()
        entry[pl.ds(pl.multiple_of((1 - k) * HALF, HALF), HALF), ln] = pin[p]
        state = entry[:, ln]
        skip_row = jnp.where(low[0:1], skip[2 * p], skip[2 * p + 1])
        for b in range(BLOCKS):
            rows = slice(b * SPAN, (b + 1) * SPAN)
            carried = dot(c_ref[rows, :], state.astype(BF16))
            ssd = (ins[rows, ln] + carried * fac[rows, ln]).astype(BF16).astype(F32)
            z = zv[rows, ln].astype(F32)
            half_z = z * 0.5
            gated = (ssd + xv[rows, ln].astype(F32) * skip_row) * (half_z + half_z * jnp.tanh(half_z))
            ins[rows, ln] = gated
            sq[rows, :] = sq[rows, :] + gated * gated
            if b < BLOCKS - 1:
                state = state * dec[b, pl.ds(p, 1), :] + adds[b, :, ln]

    def finish_step(i, _):
        @pl.when(i < PAIRS)
        def _():
            receive(serving(lax.rem(i + PAIRS - 1, PAIRS)))

        @pl.when(i + AHEAD < CHIPS - 1)
        def _():
            send_entry(i + AHEAD, 0)

        @pl.when(i >= LAG)
        def _():
            finish(serving(lax.rem(i + PAIRS - 1 - LAG, PAIRS)))

        return 0

    def to_partner(n, at, half):
        g = parts[n][1]
        if n == 0:
            return g.at[half, at]
        return g.at[half]

    def p_copy(i, arrival):
        n = 0 if i < 4 else i - 3
        at = lax.rem(y + 4 - i, 4)
        part = to_partner(n, at, 1 - k if arrival else k)
        return pltpu.make_async_remote_copy(
            src_ref=part, dst_ref=part, send_sem=gp_s.at[i], recv_sem=gp_r.at[i],
            device_id={"seq": partner}, device_id_type=MESH,
        )

    lax.fori_loop(0, SWITCH, finish_step, 0)
    for j in (1, 3):
        row_arrive(j)
        y_send(j)
    lax.fori_loop(SWITCH, PASS, finish_step, 0)
    row_arrive(2)
    y_send(2)
    p_copy(0, False).start()
    for n in (1, 2):
        stage_arrive(n, 1)
        stage_send(n, 2)
    lax.fori_loop(PASS, PAIRS + LAG, finish_step, 0)

    for b in range(BLOCKS):
        rows = slice(b * SPAN, (b + 1) * SPAN)
        mean = jnp.sum(sq[rows, :], axis=1, keepdims=True) * (1.0 / WIDE)
        inverse = jnp.broadcast_to(lax.rsqrt(mean + 1e-05), (SPAN, 128))

        def norm_step(p, _, rows=rows, inverse=inverse):
            ln = lanes_of(p)
            ob[rows, ln] = (ins[rows, ln] * inverse * gain[pl.ds(p, 1), :]).astype(BF16)
            return 0

        lax.fori_loop(0, PAIRS, norm_step, 0)

    for n in (1, 2):
        stage_arrive(n, 2)
        p_copy(3 + n, False).start()
    for j in (1, 3, 2):
        for r in range(4):
            y_copy(r, j, True).wait_recv()
        p_copy(j, False).start()
    held_copy.wait()
    for n in (1, 2):
        for stage in range(3):
            for j in range(1, 4):
                stage_copy(n, stage, j, False).wait_send()
    for r in range(4):
        for j in range(1, 4):
            y_copy(r, j, False).wait_send()
    for i in range(6):
        p_copy(i, False).wait_send()
        p_copy(i, True).wait_recv()

    def drain(p, _):
        partner_copy(p).wait_send()
        entry_to_partner(p).wait_send()

        @pl.when(p != c)
        def _():
            owner_copy(p).wait_send()
            entry_copy(p).wait_send()
            plane_copy(p).wait_send()

        return 0

    lax.fori_loop(0, PAIRS, drain, 0)


def run_mixer(values, gate, input_map, output_map, rates, steps, skip, gain, cache):
    vm = lambda *shape: pltpu.VMEM(shape, F32)
    dma = lambda *shape: pltpu.SemaphoreType.DMA(shape)
    any_spec = pl.BlockSpec(memory_space=pl.ANY)
    vmem_spec = pl.BlockSpec(memory_space=pltpu.VMEM)
    return pl.pallas_call(
        mixer_kernel,
        out_shape=(
            pltpu.VMEM((TOKENS, WIDE), BF16),
            pltpu.VMEM((GROUPS, 4, 4, 128, STATE), BF16),
            jax.ShapeDtypeStruct((2, GROUPS, 4, 4, CUT_B, HALF), BF16),
            jax.ShapeDtypeStruct((2, GROUPS, 4, 4, CUT_C - CUT_B, HALF), BF16),
            jax.ShapeDtypeStruct((2, GROUPS, 4, 4, 128 - CUT_C, HALF), BF16),
        ),
        in_specs=[any_spec, any_spec] + [vmem_spec] * 4 + [pl.BlockSpec(memory_space=pltpu.SMEM), vmem_spec, any_spec],
        out_specs=(vmem_spec, vmem_spec) + (any_spec,) * 3,
        scratch_shapes=[
            pltpu.VMEM((TOKENS, WIDE), BF16),
            pltpu.VMEM((TOKENS, WIDE), BF16),
            vm(BLOCKS - 1, STATE, WIDE),
            vm(TOKENS, WIDE),
            vm(TOKENS, WIDE),
            vm(PAIRS, 2, ROWS, 128),
            vm(PAIRS, ROWS, 128),
            vm(PAIRS, ROWS, 128),
            vm(CHIPS, ROWS, 128),
            vm(CHIPS, HALF, 128),
            vm(PAIRS, HALF, 128),
            vm(PAIRS, HALF, 128),
            vm(PAIRS, HALF, 128),
            vm(STATE, WIDE),
            vm(BLOCKS, STATE, SPAN),
            vm(BLOCKS, SPAN, SPAN),
            pltpu.VMEM((TOKENS, 128), BF16),
            vm(2, TOKENS, 256),
            pltpu.VMEM((2, BLOCKS, 256, 128), BF16),
            pltpu.VMEM((2, BLOCKS, 256, 256), BF16),
            vm(LOCAL_HEADS, TOKENS),
            vm(LOCAL_HEADS, TOKENS),
            vm(LOCAL_HEADS, TOKENS),
            vm(LOCAL_HEADS, 128),
            vm(BLOCKS, PAIRS, 128),
            vm(PAIRS, 128),
            vm(TOKENS, 128),
            pltpu.VMEM((128, HALF), BF16),
            dma(PAIRS), pltpu.SemaphoreType.DMA,
            dma(PAIRS), dma(PAIRS),
            dma(PAIRS), dma(PAIRS),
            dma(PAIRS), dma(PAIRS),
            dma(PAIRS), dma(PAIRS),
            dma(3),
            dma(3, 3), dma(3, 3), dma(3, 3), dma(3, 3), dma(3, 3), dma(3, 3), dma(4, 3), dma(4, 3), dma(CHIPS), dma(CHIPS), dma(6), dma(6),
            pltpu.SemaphoreType.DMA,
        ],
        compiler_params=pltpu.CompilerParams(
            collective_id=0, has_side_effects=True, vmem_limit_bytes=54 * 1024 * 1024
        ),
        cost_estimate=pl.CostEstimate(flops=6_000_000_000, bytes_accessed=24_000_000, transcendentals=12_000_000),
        name="mixer",
    )(values, gate, input_map, output_map, rates, steps, skip, gain, cache)


def place_kernel(slot_map, held, rows_in, ga, gb, gc, out, rows_out, buf, hin, cout, rout):
    rank = lax.axis_index("seq") * GROUPS + lax.axis_index("head")

    def final_in(g):
        for h in range(2):
            for n, (part, start, stop) in enumerate(
                ((ga, 0, CUT_B), (gb, CUT_B, CUT_C), (gc, CUT_C, 128))
            ):
                yield pltpu.make_async_copy(
                    part.at[h, g],
                    buf.at[g, :, :, pl.ds(start, stop - start), pl.ds(h * HALF, HALF)],
                    hin.at[g, 3 * h + n],
                )

    def rows_copy(b):
        rows = pl.ds(b * SPAN, SPAN)
        return pltpu.make_async_copy(rows_in.at[rows], rows_out.at[rows], rout.at[b])

    for g in range(GROUPS):
        hit = slot_map[g] == rank

        @pl.when(hit)
        def _(g=g):
            for copy in final_in(g):
                copy.start()

        @pl.when(jnp.logical_not(hit))
        def _(g=g):
            pltpu.make_async_copy(held.at[g], out.at[g], cout.at[g]).start()

        rows_copy(g).start()

    for g in range(GROUPS):
        hit = slot_map[g] == rank

        @pl.when(hit)
        def _(g=g):
            for copy in final_in(g):
                copy.wait()
            pltpu.make_async_copy(buf.at[g], out.at[g], cout.at[g]).start()

    for g in range(GROUPS):
        pltpu.make_async_copy(held.at[g], out.at[g], cout.at[g]).wait()
        rows_copy(g).wait()


def run_place(slot_map, held, rows, ga, gb, gc):
    any_spec = pl.BlockSpec(memory_space=pl.ANY)
    vmem_spec = pl.BlockSpec(memory_space=pltpu.VMEM)
    return pl.pallas_call(
        place_kernel,
        out_shape=(
            jax.ShapeDtypeStruct((GROUPS, 4, 4, 128, STATE), BF16),
            jax.ShapeDtypeStruct((TOKENS, WIDE), BF16),
        ),
        in_specs=[pl.BlockSpec(memory_space=pltpu.SMEM), vmem_spec, vmem_spec] + [any_spec] * 3,
        out_specs=(any_spec, any_spec),
        scratch_shapes=[
            pltpu.VMEM((GROUPS, 4, 4, 128, STATE), BF16),
            pltpu.SemaphoreType.DMA((GROUPS, 6)),
            pltpu.SemaphoreType.DMA((GROUPS,)),
            pltpu.SemaphoreType.DMA((GROUPS,)),
        ],
        compiler_params=pltpu.CompilerParams(vmem_limit_bytes=16 * 1024 * 1024),
        name="place",
    )(slot_map, held, rows, ga, gb, gc)


def shards(
    values, gate_rows, input_map, output_map, decay_rate, step_size, skip_gain, norm_gain, slot_map, state_cache
):
    gain = norm_gain.reshape(PAIRS, 128)
    cache = state_cache.reshape(GROUPS, 4, 4, 128, STATE)
    rows, held, ga, gb, gc = run_mixer(
        values, gate_rows, input_map, output_map, decay_rate.T, step_size.T, skip_gain, gain, cache
    )
    held, rows = (pltpu.with_memory_space_constraint(a, pltpu.VMEM) for a in (held, rows))
    ga, gb, gc = (pltpu.with_memory_space_constraint(a, pltpu.HBM) for a in (ga, gb, gc))
    new_cache, mixed_rows = run_place(slot_map, held, rows, ga, gb, gc)
    return mixed_rows, new_cache.reshape(state_cache.shape)


def solution(mesh):
    return jax.shard_map(
        shards,
        mesh=mesh,
        in_specs=(
            P("seq", "head"),
            P("seq", "head"),
            P("seq", "head"),
            P("seq", "head"),
            P("seq", "head"),
            P("seq", "head"),
            P("head"),
            P("head"),
            P(),
            P(("seq", "head"), None, None, None),
        ),
        out_specs=(P("seq", "head"), P(("seq", "head"), None, None, None)),
        check_vma=False,
    )
```

```python
import functools

import jax
import jax.numpy as jnp
from jax import lax
from jax.experimental import pallas as pl
from jax.experimental.pallas import tpu as pltpu
from jax.sharding import PartitionSpec as P

MESH = pl.DeviceIdType.MESH
F32 = jnp.float32
BF16 = jnp.bfloat16

HEADS = 128
HEAD_DIM = 64
STATE = 256
GROUPS = 4
SPAN = 256
BLOCKS = 4
TOKENS = SPAN * BLOCKS
LOCAL_HEADS = 32
PAIRS = 16
CHIPS = 16
HALF = 128
ROWS = HALF + 8
WIDE = PAIRS * 128
LOG2E = 1.4426950408889634
LAG = 3
TOP = 127.9999
EARLY = 7
AHEAD = 6
MIDDLE = 1
STOPS = (3, 4, 5, 8)
CUT_B, CUT_C = 96, 112


def dot(a, b):
    return jnp.dot(a, b, preferred_element_type=F32)


def lanes_of(p):
    return pl.ds(pl.multiple_of(p * 128, 128), 128)


ROUTE = (
    (2, 2), (1, 2), (2, 1), (3, 2), (2, 3), (1, 1), (3, 3), (1, 3), (3, 1),
    (2, 0), (0, 2), (1, 0), (0, 1), (3, 0), (0, 3), (0, 0),
)


def pick_step(i, which):
    step = ROUTE[0][which]
    for j in range(1, len(ROUTE)):
        step = jnp.where(i == j, ROUTE[j][which], step)
    return step


def mixer_kernel(
    values, gate, b_ref, c_ref, rates, steps, skip, gain, cache,
    ob, held, ga, gb, gc,
    xv, zv, adds, ins, fac, sbuf, prt, cbuf, own_in, ebuf, ent_in, mbuf, pin, entry,
    bt, ip, rcol, minus, wtop, wlow, run_t, step_t, trail_t, dwide, dec, ddec, sq, fin,
    xsem, zsem, ps_s, ps_r, os_s, os_r, en_s, en_r, ms_s, ms_r,
    gl_s, g1_s, g1_r, g2_s, g2_r, g3_s, g3_r, gy_s, gy_r, gd_s, gd_r, gp_s, gp_r, held_sem,
):
    seq = lax.axis_index("seq")
    y = lax.axis_index("head")
    c = seq // 2
    k = lax.rem(seq, 2)
    zc = lax.rem(c, 4)
    xc = c // 4
    partner = 2 * c + 1 - k

    def served(i):
        return lax.rem(xc + pick_step(i, 0), 4) * 4 + lax.rem(zc + pick_step(i, 1), 4)

    def serving(i):
        return lax.rem(xc + 4 - pick_step(i, 0), 4) * 4 + lax.rem(zc + 4 - pick_step(i, 1), 4)

    first = k == 0

    def x_copy(p):
        return pltpu.make_async_copy(values.at[:, lanes_of(p)], xv.at[:, lanes_of(p)], xsem.at[p])

    def start_x(i, _):
        x_copy(served(i)).start()
        return 0

    lax.fori_loop(0, PAIRS, start_x, 0)
    barrier = pltpu.get_barrier_semaphore()
    pl.semaphore_signal(barrier, inc=1, device_id={"seq": partner}, device_id_type=MESH)

    def greet(i, _):
        peer = lax.rem(c + 1 + i, CHIPS)
        pl.semaphore_signal(barrier, inc=1, device_id={"seq": 2 * peer + k}, device_id_type=MESH)
        return 0

    lax.fori_loop(0, CHIPS - 1, greet, 0)
    for j in range(1, GROUPS):
        pl.semaphore_signal(
            barrier, inc=1, device_id={"head": lax.rem(y + j, GROUPS)}, device_id_type=MESH
        )

    z_copy = pltpu.make_async_copy(gate, zv, zsem)
    held_copy = pltpu.make_async_copy(cache, held, held_sem)

    lane = lax.broadcasted_iota(jnp.int32, (SPAN, 128), 1)
    low = lane < 64
    upper = (
        lax.broadcasted_iota(jnp.int32, (SPAN, SPAN), 0)
        <= lax.broadcasted_iota(jnp.int32, (SPAN, SPAN), 1)
    ).astype(BF16)
    causal = (
        lax.broadcasted_iota(jnp.int32, (SPAN, SPAN), 0)
        >= lax.broadcasted_iota(jnp.int32, (SPAN, SPAN), 1)
    )
    low16 = lax.broadcasted_iota(jnp.int32, (PAIRS, 128), 1) < 64
    for b in range(BLOCKS):
        rows = slice(b * SPAN, (b + 1) * SPAN)
        run_b = dot(rates[:, rows], upper) * LOG2E
        step_b = steps[:, rows].astype(F32)
        parts, rest = [], -run_b
        for _ in range(3):
            parts.append(rest.astype(BF16).astype(F32))
            rest = rest - parts[-1]
        parts.append(jnp.zeros((128 - 3 * LOCAL_HEADS, SPAN), F32))
        rcol[rows, :] = jnp.concatenate(parts, axis=0).T.astype(BF16)
        total = run_b[:, SPAN - 1 : SPAN]
        run_t[:, rows] = run_b
        step_t[:, rows] = step_b
        trail_t[:, rows] = jnp.exp2(run_b - total) * step_b
        dwide[...] = jnp.broadcast_to(jnp.exp2(-total), (LOCAL_HEADS, 128))
        part = jnp.where(low16, dwide[pl.ds(0, PAIRS, 2), :], dwide[pl.ds(1, PAIRS, 2), :])
        dec[b] = part
        ddec[...] = part if b == 0 else ddec[...] * part
        bt[b] = b_ref[rows, :].astype(F32).T
        inner_prod = lax.dot_general(
            c_ref[rows, :], b_ref[rows, :], (((1,), (1,)), ((), ())), preferred_element_type=F32
        )
        ip[b] = jnp.where(causal, inner_prod, 0.0)

    def partner_copy(p):
        return pltpu.make_async_remote_copy(
            src_ref=sbuf.at[p, 1 - k], dst_ref=prt.at[p], send_sem=ps_s.at[p], recv_sem=ps_r.at[p],
            device_id={"seq": partner}, device_id_type=MESH,
        )

    def owner_copy(p):
        return pltpu.make_async_remote_copy(
            src_ref=cbuf.at[p], dst_ref=own_in.at[c], send_sem=os_s.at[p], recv_sem=os_r.at[c],
            device_id={"seq": 2 * p + k}, device_id_type=MESH,
        )

    def owner_arrival(j):
        return pltpu.make_async_remote_copy(
            src_ref=cbuf.at[j], dst_ref=own_in.at[j], send_sem=os_s.at[j], recv_sem=os_r.at[j],
            device_id={"seq": 2 * j + k}, device_id_type=MESH,
        )

    def states(p):
        ln = lanes_of(p)
        state = None
        for b in range(BLOCKS):
            rows = slice(b * SPAN, (b + 1) * SPAN)
            x = xv[rows, ln]
            wide = bt[b]
            s0 = (wide * trail_t[pl.ds(2 * p, 1), rows]).astype(BF16)
            s1 = (wide * trail_t[pl.ds(2 * p + 1, 1), rows]).astype(BF16)
            add = jnp.where(low, dot(s0, x), dot(s1, x))
            if b < BLOCKS - 1:
                adds[b, :, ln] = add
            state = add if b == 0 else state * dec[b, pl.ds(p, 1), :] + add
        decay = jnp.broadcast_to(ddec[pl.ds(p, 1), :], (8, 128))
        for h in range(2):
            sbuf[p, h, 0:HALF, :] = state[h * HALF : (h + 1) * HALF]
            sbuf[p, h, HALF:ROWS, :] = decay

    def combine(p):
        partner_copy(p).wait_recv()
        here = sbuf[p, k]
        there = prt[p]
        early = jnp.where(first, here, there)
        late = jnp.where(first, there, here)
        decay = late[HALF : HALF + 1, :]
        return early[0:HALF] * decay + late[0:HALF], early[HALF:ROWS] * late[HALF:ROWS]

    def send_owner(p):
        both, decay = combine(p)
        cbuf[p, 0:HALF, :] = both
        cbuf[p, HALF:ROWS, :] = decay
        owner_copy(p).start()

    def states_step(i, _):
        first_p, second_p = served(2 * i), served(2 * i + 1)
        x_copy(first_p).wait()
        x_copy(second_p).wait()
        states(first_p)
        states(second_p)

        @pl.when(i == 0)
        def _():
            pl.semaphore_wait(barrier, 1 + (CHIPS - 1) + (GROUPS - 1))

        partner_copy(first_p).start()
        partner_copy(second_p).start()

        @pl.when(i >= 1)
        def _():
            send_owner(served(2 * i - 2))
            send_owner(served(2 * i - 1))

        return 0

    lax.fori_loop(0, PAIRS // 2, states_step, 0)
    z_copy.start()
    held_copy.start()
    send_owner(served(PAIRS - 2))
    both, decay = combine(c)
    own_in[c, 0:HALF, :] = both
    own_in[c, HALF:ROWS, :] = decay

    row_s = lax.rem(lax.broadcasted_iota(jnp.int32, (128, 256), 0), LOCAL_HEADS)
    lane_s = lax.broadcasted_iota(jnp.int32, (128, 256), 1) // 128
    head_s = row_s - lane_s

    def spread(p, slot):
        pick = jnp.where(head_s == 2 * p, 1.0, 0.0).astype(BF16)
        for b in range(BLOCKS):
            rows = slice(b * SPAN, (b + 1) * SPAN)
            minus[slot, rows, :] = dot(rcol[rows, :], pick)

    def weigh(p, slot, b):
        ln = lanes_of(p)
        r0 = b * SPAN
        rows = slice(r0, r0 + SPAN)
        m = [minus[slot, rows, 128 * h : 128 * h + 128] for h in range(2)]
        fac[rows, ln] = jnp.exp2(jnp.where(low, m[0], m[1]))
        for h in range(2):
            ru = run_t[pl.ds(2 * p + h, 1), rows]
            st = step_t[pl.ds(2 * p + h, 1), rows]
            near = slice(128 * h, 128 * h + 128)
            w00 = jnp.exp2(jnp.minimum(ru[:, :128] + m[h][:128], TOP)) * ip[b, :128, :128] * st[:, :128]
            wtop[slot, b, near, :] = w00.astype(BF16)
            w10 = jnp.exp2(ru[:, :128] + m[h][128:]) * ip[b, 128:, :128] * st[:, :128]
            wlow[slot, b, near, 0:128] = w10.astype(BF16)
            w11 = jnp.exp2(jnp.minimum(ru[:, 128:] + m[h][128:], TOP)) * ip[b, 128:, 128:] * st[:, 128:]
            wlow[slot, b, near, 128:256] = w11.astype(BF16)

    def apply(p, slot, b):
        ln = lanes_of(p)
        r0 = b * SPAN
        x = xv[r0 : r0 + SPAN, ln]
        top = dot(wtop[slot, b], x[:128])
        bottom = dot(wlow[slot, b], x)
        ins[r0 : r0 + 128, ln] = jnp.where(low[:128], top[:128], top[128:])
        ins[r0 + 128 : r0 + 256, ln] = jnp.where(low[:128], bottom[:128], bottom[128:])

    def inner(i, _):
        p0, p1 = 2 * i, 2 * i + 1
        old = lax.rem(p1 + PAIRS - 2, PAIRS)
        for b in range(BLOCKS):
            apply(old, 1, b)
            weigh(p0, 0, b)
        spread(lax.rem(p0 + 2, PAIRS), 0)
        for b in range(BLOCKS):
            apply(p0, 0, b)
            weigh(p1, 1, b)
        spread(lax.rem(p1 + 2, PAIRS), 1)
        return 0

    wtop[1] = jnp.zeros_like(wtop[1])
    wlow[1] = jnp.zeros_like(wlow[1])
    spread(0, 0)
    spread(1, 1)
    lax.fori_loop(0, EARLY, inner, 0)

    def scan_step(j, state):
        @pl.when(j != c)
        def _():
            owner_arrival(j).wait_recv()

        ebuf[j] = state
        return state * own_in[j, HALF : HALF + 1, :] + own_in[j, 0:HALF, :]

    last = lax.fori_loop(0, CHIPS, scan_step, jnp.zeros((HALF, 128), F32))
    fin[...] = last.T.astype(BF16)

    rows_a, rows_b, rows_c = pl.ds(0, CUT_B), pl.ds(CUT_B, CUT_C - CUT_B), pl.ds(CUT_C, 128 - CUT_C)
    parts = ((rows_a, ga, "xzy"), (rows_b, gb, "yzx"), (rows_c, gc, "yxz"))

    def keep(n):
        rows, g, _ = parts[n]
        return pltpu.make_async_copy(fin.at[rows], g.at[k, y, xc, zc], gl_s.at[n])

    def peer(axis, j):
        if axis == "y":
            return {"head": lax.rem(y + j, 4)}
        if axis == "x":
            return {"seq": 2 * (lax.rem(xc + j, 4) * 4 + zc) + k}
        return {"seq": 2 * (xc * 4 + lax.rem(zc + j, 4)) + k}

    def region(g, done, axis, j):
        at = {"y": y, "x": xc, "z": zc}
        if j:
            at[axis] = lax.rem(at[axis] + 4 - j, 4)
        index = [k] + [slice(None) if a in done else at[a] for a in "yxz"]
        return g.at[tuple(index)]

    def stage_copy(n, stage, j, arrival):
        rows, g, order = parts[n]
        axis = order[stage]
        there = region(g, order[:stage], axis, j if arrival else 0)
        source = fin.at[rows] if stage == 0 else there
        sem_s, sem_r = ((g1_s, g1_r), (g2_s, g2_r), (g3_s, g3_r))[stage]
        return pltpu.make_async_remote_copy(
            src_ref=source, dst_ref=there, send_sem=sem_s.at[n, j - 1], recv_sem=sem_r.at[n, j - 1],
            device_id=peer(axis, j), device_id_type=MESH,
        )

    def stage_send(n, stage):
        for j in (1, 3, 2):
            stage_copy(n, stage, j, False).start()

    def stage_arrive(n, stage):
        for j in (1, 3, 2):
            stage_copy(n, stage, j, True).wait_recv()

    def y_copy(r, j, arrival):
        there = ga.at[k, lax.rem(y + 4 - j, 4) if arrival else y, lax.rem(xc + 4 - r, 4)]
        return pltpu.make_async_remote_copy(
            src_ref=there, dst_ref=there, send_sem=gy_s.at[r, j - 1], recv_sem=gy_r.at[r, j - 1],
            device_id=peer("y", j), device_id_type=MESH,
        )

    def plane_copy(d):
        return pltpu.make_async_remote_copy(
            src_ref=fin.at[rows_a], dst_ref=ga.at[k, y, xc, zc], send_sem=gd_s.at[d], recv_sem=gd_r.at[c],
            device_id={"seq": 2 * d + k}, device_id_type=MESH,
        )

    def plane_arrival(d):
        return pltpu.make_async_remote_copy(
            src_ref=fin.at[rows_a], dst_ref=ga.at[k, y, d // 4, lax.rem(d, 4)],
            send_sem=gd_s.at[d], recv_sem=gd_r.at[d],
            device_id={"seq": 2 * d + k}, device_id_type=MESH,
        )

    def plane_send(i, _):
        plane_copy(served(i)).start()
        return 0

    def row_arrive(r):
        def step(i, _):
            d = lax.rem(xc + 4 - r, 4) * 4 + i

            @pl.when(d != c)
            def _():
                plane_arrival(d).wait_recv()

            return 0

        lax.fori_loop(0, 4, step, 0)

    def y_send(r):
        for j in (1, 3, 2):
            y_copy(r, j, False).start()

    for n in range(3):
        keep(n).start()
    for n in (1, 2):
        stage_send(n, 0)
    lax.fori_loop(0, CHIPS - 1, plane_send, 0)

    def entry_copy(j):
        return pltpu.make_async_remote_copy(
            src_ref=ebuf.at[j], dst_ref=ent_in.at[c], send_sem=en_s.at[j], recv_sem=en_r.at[c],
            device_id={"seq": 2 * j + k}, device_id_type=MESH,
        )

    def entry_arrival(p):
        return pltpu.make_async_remote_copy(
            src_ref=ebuf.at[p], dst_ref=ent_in.at[p], send_sem=en_s.at[p], recv_sem=en_r.at[p],
            device_id={"seq": 2 * p + k}, device_id_type=MESH,
        )

    def send_entry(i, _):
        entry_copy(served(i)).start()
        return 0

    lax.fori_loop(0, AHEAD, send_entry, 0)
    lax.fori_loop(EARLY, EARLY + MIDDLE, inner, 0)
    for n in range(3):
        keep(n).wait()
    for n in (1, 2):
        stage_arrive(n, 0)
        stage_send(n, 1)
    row_arrive(0)
    y_send(0)
    ent_in[c] = ebuf[c]

    lax.fori_loop(EARLY + MIDDLE, PAIRS // 2, inner, 0)
    for b in range(BLOCKS):
        apply(PAIRS - 1, 1, b)

    def entry_to_partner(p):
        return pltpu.make_async_remote_copy(
            src_ref=mbuf.at[p], dst_ref=pin.at[p], send_sem=ms_s.at[p], recv_sem=ms_r.at[p],
            device_id={"seq": partner}, device_id_type=MESH,
        )

    z_copy.wait()
    sq[...] = jnp.zeros_like(sq)

    def receive(p):
        @pl.when(p != c)
        def _():
            entry_arrival(p).wait_recv()

        state = ent_in[p]
        early = jnp.where(first, sbuf[p, 0], prt[p])
        moved = state * early[HALF : HALF + 1, :] + early[0:HALF]
        entry[pl.ds(pl.multiple_of(k * HALF, HALF), HALF), lanes_of(p)] = jnp.where(first, state, moved)
        mbuf[p] = jnp.where(first, moved, state)
        entry_to_partner(p).start()

    def finish(p):
        ln = lanes_of(p)
        entry_to_partner(p).wait_recv()
        entry[pl.ds(pl.multiple_of((1 - k) * HALF, HALF), HALF), ln] = pin[p]
        state = entry[:, ln]
        skip_row = jnp.where(low[0:1], skip[2 * p], skip[2 * p + 1])
        for b in range(BLOCKS):
            rows = slice(b * SPAN, (b + 1) * SPAN)
            carried = dot(c_ref[rows, :], state.astype(BF16))
            ssd = (ins[rows, ln] + carried * fac[rows, ln]).astype(BF16).astype(F32)
            z = zv[rows, ln].astype(F32)
            half_z = z * 0.5
            gated = (ssd + xv[rows, ln].astype(F32) * skip_row) * (half_z + half_z * jnp.tanh(half_z))
            ins[rows, ln] = gated
            sq[rows, :] = sq[rows, :] + gated * gated
            if b < BLOCKS - 1:
                state = state * dec[b, pl.ds(p, 1), :] + adds[b, :, ln]

    def finish_step(i, _):
        @pl.when(i < PAIRS)
        def _():
            receive(serving(lax.rem(i + PAIRS - 1, PAIRS)))

        @pl.when(i + AHEAD < CHIPS - 1)
        def _():
            send_entry(i + AHEAD, 0)

        @pl.when(i >= LAG)
        def _():
            finish(serving(lax.rem(i + PAIRS - 1 - LAG, PAIRS)))

        return 0

    def to_partner(n, at, half):
        g = parts[n][1]
        if n == 0:
            return g.at[half, at]
        return g.at[half]

    def p_copy(i, arrival):
        n = 0 if i < 4 else i - 3
        at = lax.rem(y + 4 - i, 4)
        part = to_partner(n, at, 1 - k if arrival else k)
        return pltpu.make_async_remote_copy(
            src_ref=part, dst_ref=part, send_sem=gp_s.at[i], recv_sem=gp_r.at[i],
            device_id={"seq": partner}, device_id_type=MESH,
        )

    done = 0
    for n, r in enumerate((1, 3, 2)):
        lax.fori_loop(done, STOPS[n], finish_step, 0)
        done = STOPS[n]
        row_arrive(r)
        y_send(r)
    p_copy(0, False).start()
    lax.fori_loop(done, STOPS[3], finish_step, 0)
    for n in (1, 2):
        stage_arrive(n, 1)
        stage_send(n, 2)
    lax.fori_loop(STOPS[3], PAIRS + LAG, finish_step, 0)

    for b in range(BLOCKS):
        rows = slice(b * SPAN, (b + 1) * SPAN)
        mean = jnp.sum(sq[rows, :], axis=1, keepdims=True) * (1.0 / WIDE)
        inverse = jnp.broadcast_to(lax.rsqrt(mean + 1e-05), (SPAN, 128))

        def norm_step(p, _, rows=rows, inverse=inverse):
            ln = lanes_of(p)
            ob[rows, ln] = (ins[rows, ln] * inverse * gain[pl.ds(p, 1), :]).astype(BF16)
            return 0

        lax.fori_loop(0, PAIRS, norm_step, 0)

    for n in (1, 2):
        stage_arrive(n, 2)
        p_copy(3 + n, False).start()
    for j in (1, 3, 2):
        for r in range(4):
            y_copy(r, j, True).wait_recv()
        p_copy(j, False).start()
    held_copy.wait()
    for n in (1, 2):
        for stage in range(3):
            for j in range(1, 4):
                stage_copy(n, stage, j, False).wait_send()
    for r in range(4):
        for j in range(1, 4):
            y_copy(r, j, False).wait_send()
    for i in range(6):
        p_copy(i, False).wait_send()
        p_copy(i, True).wait_recv()

    def drain(p, _):
        partner_copy(p).wait_send()
        entry_to_partner(p).wait_send()

        @pl.when(p != c)
        def _():
            owner_copy(p).wait_send()
            entry_copy(p).wait_send()
            plane_copy(p).wait_send()

        return 0

    lax.fori_loop(0, PAIRS, drain, 0)


def run_mixer(values, gate, input_map, output_map, rates, steps, skip, gain, cache):
    vm = lambda *shape: pltpu.VMEM(shape, F32)
    dma = lambda *shape: pltpu.SemaphoreType.DMA(shape)
    any_spec = pl.BlockSpec(memory_space=pl.ANY)
    vmem_spec = pl.BlockSpec(memory_space=pltpu.VMEM)
    return pl.pallas_call(
        mixer_kernel,
        out_shape=(
            pltpu.VMEM((TOKENS, WIDE), BF16),
            pltpu.VMEM((GROUPS, 4, 4, 128, STATE), BF16),
            jax.ShapeDtypeStruct((2, GROUPS, 4, 4, CUT_B, HALF), BF16),
            jax.ShapeDtypeStruct((2, GROUPS, 4, 4, CUT_C - CUT_B, HALF), BF16),
            jax.ShapeDtypeStruct((2, GROUPS, 4, 4, 128 - CUT_C, HALF), BF16),
        ),
        in_specs=[any_spec, any_spec] + [vmem_spec] * 4 + [pl.BlockSpec(memory_space=pltpu.SMEM), vmem_spec, any_spec],
        out_specs=(vmem_spec, vmem_spec) + (any_spec,) * 3,
        scratch_shapes=[
            pltpu.VMEM((TOKENS, WIDE), BF16),
            pltpu.VMEM((TOKENS, WIDE), BF16),
            vm(BLOCKS - 1, STATE, WIDE),
            vm(TOKENS, WIDE),
            vm(TOKENS, WIDE),
            vm(PAIRS, 2, ROWS, 128),
            vm(PAIRS, ROWS, 128),
            vm(PAIRS, ROWS, 128),
            vm(CHIPS, ROWS, 128),
            vm(CHIPS, HALF, 128),
            vm(PAIRS, HALF, 128),
            vm(PAIRS, HALF, 128),
            vm(PAIRS, HALF, 128),
            vm(STATE, WIDE),
            vm(BLOCKS, STATE, SPAN),
            vm(BLOCKS, SPAN, SPAN),
            pltpu.VMEM((TOKENS, 128), BF16),
            vm(2, TOKENS, 256),
            pltpu.VMEM((2, BLOCKS, 256, 128), BF16),
            pltpu.VMEM((2, BLOCKS, 256, 256), BF16),
            vm(LOCAL_HEADS, TOKENS),
            vm(LOCAL_HEADS, TOKENS),
            vm(LOCAL_HEADS, TOKENS),
            vm(LOCAL_HEADS, 128),
            vm(BLOCKS, PAIRS, 128),
            vm(PAIRS, 128),
            vm(TOKENS, 128),
            pltpu.VMEM((128, HALF), BF16),
            dma(PAIRS), pltpu.SemaphoreType.DMA,
            dma(PAIRS), dma(PAIRS),
            dma(PAIRS), dma(PAIRS),
            dma(PAIRS), dma(PAIRS),
            dma(PAIRS), dma(PAIRS),
            dma(3),
            dma(3, 3), dma(3, 3), dma(3, 3), dma(3, 3), dma(3, 3), dma(3, 3), dma(4, 3), dma(4, 3), dma(CHIPS), dma(CHIPS), dma(6), dma(6),
            pltpu.SemaphoreType.DMA,
        ],
        compiler_params=pltpu.CompilerParams(
            collective_id=0, has_side_effects=True, vmem_limit_bytes=54 * 1024 * 1024
        ),
        cost_estimate=pl.CostEstimate(flops=6_000_000_000, bytes_accessed=24_000_000, transcendentals=12_000_000),
        name="mixer",
    )(values, gate, input_map, output_map, rates, steps, skip, gain, cache)


def place_kernel(slot_map, held, rows_in, ga, gb, gc, out, rows_out, buf, hin, cout, rout):
    rank = lax.axis_index("seq") * GROUPS + lax.axis_index("head")

    def final_in(g):
        for h in range(2):
            for n, (part, start, stop) in enumerate(
                ((ga, 0, CUT_B), (gb, CUT_B, CUT_C), (gc, CUT_C, 128))
            ):
                yield pltpu.make_async_copy(
                    part.at[h, g],
                    buf.at[g, :, :, pl.ds(start, stop - start), pl.ds(h * HALF, HALF)],
                    hin.at[g, 3 * h + n],
                )

    def rows_copy(b):
        rows = pl.ds(b * SPAN, SPAN)
        return pltpu.make_async_copy(rows_in.at[rows], rows_out.at[rows], rout.at[b])

    for g in range(GROUPS):
        hit = slot_map[g] == rank

        @pl.when(hit)
        def _(g=g):
            for copy in final_in(g):
                copy.start()

        @pl.when(jnp.logical_not(hit))
        def _(g=g):
            pltpu.make_async_copy(held.at[g], out.at[g], cout.at[g]).start()

        rows_copy(g).start()

    for g in range(GROUPS):
        hit = slot_map[g] == rank

        @pl.when(hit)
        def _(g=g):
            for copy in final_in(g):
                copy.wait()
            pltpu.make_async_copy(buf.at[g], out.at[g], cout.at[g]).start()

    for g in range(GROUPS):
        pltpu.make_async_copy(held.at[g], out.at[g], cout.at[g]).wait()
        rows_copy(g).wait()


def run_place(slot_map, held, rows, ga, gb, gc):
    any_spec = pl.BlockSpec(memory_space=pl.ANY)
    vmem_spec = pl.BlockSpec(memory_space=pltpu.VMEM)
    return pl.pallas_call(
        place_kernel,
        out_shape=(
            jax.ShapeDtypeStruct((GROUPS, 4, 4, 128, STATE), BF16),
            jax.ShapeDtypeStruct((TOKENS, WIDE), BF16),
        ),
        in_specs=[pl.BlockSpec(memory_space=pltpu.SMEM), vmem_spec, vmem_spec] + [any_spec] * 3,
        out_specs=(any_spec, any_spec),
        scratch_shapes=[
            pltpu.VMEM((GROUPS, 4, 4, 128, STATE), BF16),
            pltpu.SemaphoreType.DMA((GROUPS, 6)),
            pltpu.SemaphoreType.DMA((GROUPS,)),
            pltpu.SemaphoreType.DMA((GROUPS,)),
        ],
        compiler_params=pltpu.CompilerParams(vmem_limit_bytes=16 * 1024 * 1024),
        name="place",
    )(slot_map, held, rows, ga, gb, gc)


def shards(
    values, gate_rows, input_map, output_map, decay_rate, step_size, skip_gain, norm_gain, slot_map, state_cache
):
    gain = norm_gain.reshape(PAIRS, 128)
    cache = state_cache.reshape(GROUPS, 4, 4, 128, STATE)
    rows, held, ga, gb, gc = run_mixer(
        values, gate_rows, input_map, output_map, decay_rate.T, step_size.T, skip_gain, gain, cache
    )
    held, rows = (pltpu.with_memory_space_constraint(a, pltpu.VMEM) for a in (held, rows))
    ga, gb, gc = (pltpu.with_memory_space_constraint(a, pltpu.HBM) for a in (ga, gb, gc))
    new_cache, mixed_rows = run_place(slot_map, held, rows, ga, gb, gc)
    return mixed_rows, new_cache.reshape(state_cache.shape)


def solution(mesh):
    return jax.shard_map(
        shards,
        mesh=mesh,
        in_specs=(
            P("seq", "head"),
            P("seq", "head"),
            P("seq", "head"),
            P("seq", "head"),
            P("seq", "head"),
            P("seq", "head"),
            P("head"),
            P("head"),
            P(),
            P(("seq", "head"), None, None, None),
        ),
        out_specs=(P("seq", "head"), P(("seq", "head"), None, None, None)),
        check_vma=False,
    )
```
